32 devices in a mesh: frame: 8 (over y, x, core), qblk: 4 (over z).
Axes of the slice: x: 2, y: 2, z: 4, core: 2. Of those that a mesh axis runs over, the one named last changes fastest.
Arguments:
- query_tokens: bfloat16 [8, 144, 768], P('frame', 'qblk'), may hold values from -12 to 12
- key_tokens: bfloat16 [8, 144, 768], P('frame', 'qblk'), may hold values from -12 to 12
- value_tokens: bfloat16 [8, 144, 768], P('frame', 'qblk'), may hold values from -4 to 4
- w_query: bfloat16 [768, 768], replicated, as said below
- w_key: bfloat16 [768, 768], replicated, as said below
- w_value: bfloat16 [768, 768], replicated, may hold values from -0.4375 to 0.4375
Outputs:
- trajectory: bfloat16 [8, 144, 768], P('frame', 'qblk')
The draws below stay inside these ranges and needn't reach their ends.
Inputs may be any that keep to these rules, and one draw needn't show every extreme that they name: `w_query`: entries of order one over the square root of 768. `w_key`: entries of order one over the square root of 768.
All inputs are finite; a program needn't handle non-finite values.
Results may differ from the reference program's by a relative error of at most 0.0091.
Values may be sent and summed in bfloat16 or wider, within the bound.
No kernel may reach another device: no remote copies, remote signals or barrier semaphores. Data moves between devices by JAX's collectives and lax.ppermute only.
A program may use at most 64 MiB of HBM per device.

```python
import math
import jax
import jax.numpy as jnp
from jax import lax

D = 768
HEADS = 12
FRAMES = 8
S = 144


def draw_query_tokens(key, part):
    base = 3.0 * jax.random.truncated_normal(jax.random.fold_in(key, 1), -4.0, 4.0, (FRAMES, S, D), jnp.float32)
    return base.astype(jnp.bfloat16)


def draw_key_tokens(key, part):
    base = jax.random.truncated_normal(jax.random.fold_in(key, 2), -4.0, 4.0, (FRAMES, S, D), jnp.float32)
    return base.astype(jnp.bfloat16)


def draw_value_tokens(key, part):
    base = jax.random.truncated_normal(jax.random.fold_in(key, 3), -4.0, 4.0, (FRAMES, S, D), jnp.float32)
    return base.astype(jnp.bfloat16)


def weight_parts(key):
    base = jax.random.fold_in(key, 202)
    return [jax.random.truncated_normal(jax.random.fold_in(base, number), -4.0, 4.0, (D, D), jnp.float32) for number in range(3)]


def draw_w_query(key, part):
    common, first, second = weight_parts(key)
    spread = 2.2 / math.sqrt(D)
    return (first * spread).astype(jnp.bfloat16)


def draw_w_key(key, part):
    common, first, second = weight_parts(key)
    spread = 2.2 / math.sqrt(D)
    return (second * spread).astype(jnp.bfloat16)


def scatter_about(key, extent, scale, bound, held_as=jnp.bfloat16):
    values = jax.random.normal(key, extent, jnp.float32) * scale
    return jnp.minimum(jnp.maximum(values, -bound), bound).astype(held_as)


def setup_inputs(seed: int = 0) -> dict:
    seeds = jax.random.split(jax.random.key(seed), 7)
    return {
        "query_tokens": draw_query_tokens(jax.random.fold_in(seeds[6], 71), 0),
        "key_tokens": draw_key_tokens(jax.random.fold_in(seeds[6], 71), 0),
        "value_tokens": draw_value_tokens(jax.random.fold_in(seeds[6], 71), 0),
        "w_query": draw_w_query(jax.random.fold_in(seeds[6], 71), 0),
        "w_key": draw_w_key(jax.random.fold_in(seeds[6], 71), 0),
        "w_value": scatter_about(seeds[5], (D, D), (D // 4) ** -0.5, 0.4375),
    }


def pool_heads(query_rows, key_rows, value_rows):
    head_width = query_rows.shape[1] // HEADS
    scale_factor = 1.0 / math.sqrt(head_width)
    query_split = query_rows.astype(jnp.float32).reshape(-1, HEADS, head_width)
    key_split = key_rows.astype(jnp.float32).reshape(-1, HEADS, head_width)
    value_split = value_rows.astype(jnp.float32).reshape(-1, HEADS, head_width)
    scores = jnp.einsum('qhd,khd->hqk', query_split, key_split) * scale_factor
    shifted = jnp.exp(scores - lax.optimization_barrier(jnp.max(scores, axis=2, keepdims=True)))
    weights = (shifted / lax.optimization_barrier(jnp.sum(shifted, axis=2, keepdims=True))).astype(jnp.bfloat16)
    pooled = jnp.einsum('hqk,khd->qhd', weights.astype(jnp.float32), value_split)
    return pooled.reshape(query_rows.shape[0], -1).astype(jnp.bfloat16)

def project(rows, matrix):
    return jnp.dot(rows, matrix, preferred_element_type=jnp.float32).astype(jnp.bfloat16)

def trajectory_mix(query_proj, key_proj, value_proj):
    frame_count, row_count, feature_width = key_proj.shape
    head_width = feature_width // HEADS
    scale_factor = 1.0 / math.sqrt(head_width)
    query_split = query_proj.astype(jnp.float32).reshape(row_count, HEADS, head_width)
    key_split = key_proj.astype(jnp.float32).reshape(frame_count, row_count, HEADS, head_width)
    value_split = value_proj.astype(jnp.float32).reshape(frame_count, row_count, HEADS, head_width)
    scores = jnp.einsum('nhd,fnhd->nhf', query_split, key_split) * scale_factor
    shifted = jnp.exp(scores - lax.optimization_barrier(jnp.max(scores, axis=2, keepdims=True)))
    weights = (shifted / lax.optimization_barrier(jnp.sum(shifted, axis=2, keepdims=True))).astype(jnp.bfloat16)
    mixed_rows = jnp.einsum('nhf,fnhd->nhd', weights.astype(jnp.float32), value_split)
    return mixed_rows.reshape(row_count, feature_width).astype(jnp.bfloat16)

def reference(query_tokens, key_tokens, value_tokens, w_query, w_key, w_value):

    def one_frame(frame_index):
        query_rows = lax.dynamic_index_in_dim(query_tokens, frame_index, 0, keepdims=False)
        pooled = lax.map(lambda operands: pool_heads(query_rows, operands[0], operands[1]), (key_tokens, value_tokens))
        diagonal = lax.dynamic_index_in_dim(pooled, frame_index, 0, keepdims=False)
        flat_rows = pooled.reshape(-1, pooled.shape[2])
        query_proj = project(diagonal, w_query)
        key_proj = project(flat_rows, w_key).reshape(pooled.shape)
        value_proj = project(flat_rows, w_value).reshape(pooled.shape)
        return trajectory_mix(query_proj, key_proj, value_proj)
    return lax.map(one_frame, jnp.arange(FRAMES, dtype=jnp.int32))
```

```python
import functools
import math

import jax
import jax.numpy as jnp
from jax import lax
from jax.experimental import pallas as pl
from jax.experimental.pallas import tpu as pltpu
from jax.sharding import PartitionSpec as P

HEADS = 12
LANES = 128
VMEM = pl.BlockSpec(memory_space=pltpu.VMEM)
NT = (((1,), (1,)), ((), ()))


def ceil_to(value, unit):
    return -(-value // unit) * unit


def stack_rows(blocks, stage):
    rows = blocks[0].shape[0]
    pitch = ceil_to(rows, 8)
    for index, block in enumerate(blocks):
        stage[pl.ds(index * pitch, rows), :] = block.astype(jnp.float32)
        if pitch > rows:
            stage[pl.ds(index * pitch + rows, pitch - rows), :] = jnp.zeros(
                (pitch - rows, stage.shape[1]), jnp.float32
            )
    return stage[...].astype(jnp.bfloat16)


def attend(query, key, value, valid, head_width, put):
    per_slab = LANES // head_width
    factor = math.log2(math.e) / math.sqrt(head_width)
    key_total = key.shape[0]
    lane = lax.broadcasted_iota(jnp.int32, (key_total, LANES), 1) // head_width
    bias = jnp.where(valid, 0.0, -1e30)
    for slab in range(query.shape[1] // LANES):
        cut = slice(slab * LANES, (slab + 1) * LANES)
        query_slab, key_slab, value_slab = query[:, cut], key[:, cut], value[:, cut]
        total = None
        for head in range(per_slab):
            own = lane == head
            masked_key = jnp.where(own, key_slab, 0)
            scores = lax.dot_general(query_slab, masked_key, NT, preferred_element_type=jnp.float32)
            scores = scores + bias
            top = jnp.max(scores, axis=1, keepdims=True)
            weights = jnp.exp2((scores - top) * factor)
            weights = weights * (1.0 / jnp.sum(weights, axis=1, keepdims=True))
            part = jnp.dot(
                weights.astype(jnp.bfloat16),
                jnp.where(own, value_slab, 0),
                preferred_element_type=jnp.float32,
            )
            total = part if total is None else total + part
        put(slab, total)


def attention_kernel(head_width, query_count, block_count, has_earlier, *refs):
    queries = refs[:query_count]
    keys = refs[query_count : query_count + block_count]
    values = refs[query_count + block_count : query_count + 2 * block_count]
    refs = refs[query_count + 2 * block_count :]
    earlier = refs[:query_count] if has_earlier else ()
    refs = refs[len(earlier) :]
    outs, (query_stage, key_stage, value_stage) = refs[:query_count], refs[query_count:]
    rows = queries[0].shape[-2]
    pitch = ceil_to(rows, 8)
    query = stack_rows([ref[0] for ref in queries], query_stage)
    key = stack_rows([ref[0] for ref in keys], key_stage)
    value = stack_rows([ref[0] for ref in values], value_stage)
    place = lax.broadcasted_iota(jnp.int32, (1, key.shape[0]), 1)
    valid = lax.rem(place, pitch) < rows

    def put(slab, pooled):
        for index in range(query_count):
            outs[index][outs[index].shape[0] - 1, :, pl.ds(slab * LANES, LANES)] = pooled[
                index * pitch : index * pitch + rows
            ].astype(jnp.bfloat16)

    attend(query, key, value, valid, head_width, put)
    for index, ref in enumerate(earlier):
        outs[index][0] = ref[0]


def attention(queries, keys, values, earlier=()):
    _, rows, width = queries[0].shape
    pitch = ceil_to(rows, 8)
    count = len(queries)
    kernel = functools.partial(attention_kernel, width // HEADS, count, len(keys), bool(earlier))
    flops = 4 * count * rows * len(keys) * rows * width
    shape = jax.ShapeDtypeStruct((2 if earlier else 1, rows, width), jnp.bfloat16)
    return pl.pallas_call(
        kernel,
        out_shape=[shape] * count,
        in_specs=[VMEM] * (count + 2 * len(keys) + len(earlier)),
        out_specs=[VMEM] * count,
        scratch_shapes=[
            pltpu.VMEM((count * pitch, width), jnp.float32),
            pltpu.VMEM((len(keys) * pitch, width), jnp.float32),
            pltpu.VMEM((len(keys) * pitch, width), jnp.float32),
        ],
        compiler_params=pltpu.CompilerParams(vmem_limit_bytes=48 << 20),
        cost_estimate=pl.CostEstimate(flops=flops, bytes_accessed=1 << 20, transcendentals=0),
        name="attention",
    )(*queries, *keys, *values, *earlier)


def mix_kernel(head_width, pieces, *refs):
    arrived = refs[:pieces]
    w_query, w_key, w_value, out, stage, key_stage, value_stage = refs[pieces:]
    blocks = [ref[index] for ref in arrived for index in range(ref.shape[0])]
    rows, width = blocks[0].shape
    pitch = ceil_to(rows, 8)
    count = len(blocks)
    scale = 1.0 / math.sqrt(head_width)
    pooled = stack_rows(blocks, stage)
    own = pooled[:ceil_to(rows, 16)]
    query = jnp.dot(own, w_query[...], preferred_element_type=jnp.float32)[:pitch]
    query = query.astype(jnp.bfloat16).astype(jnp.float32)
    key_stage[...] = (
        jnp.dot(pooled, w_key[...], preferred_element_type=jnp.float32)
        .astype(jnp.bfloat16)
        .astype(jnp.float32)
    )
    value_stage[...] = (
        jnp.dot(pooled, w_value[...], preferred_element_type=jnp.float32)
        .astype(jnp.bfloat16)
        .astype(jnp.float32)
    )
    member = (
        lax.broadcasted_iota(jnp.int32, (width, LANES), 0) // head_width
        == lax.broadcasted_iota(jnp.int32, (width, LANES), 1)
    ).astype(jnp.bfloat16)
    spread = (
        lax.broadcasted_iota(jnp.int32, (LANES, width), 1) // head_width
        == lax.broadcasted_iota(jnp.int32, (LANES, width), 0)
    ).astype(jnp.bfloat16)
    product = jnp.concatenate(
        [key_stage[pl.ds(index * pitch, pitch), :] * query for index in range(count)], axis=0
    )
    high = product.astype(jnp.bfloat16)
    low = (product - high.astype(jnp.float32)).astype(jnp.bfloat16)
    scores = jnp.dot(high, member, preferred_element_type=jnp.float32) + jnp.dot(
        low, member, preferred_element_type=jnp.float32
    )
    scores = scores * scale
    parts = [scores[index * pitch : (index + 1) * pitch] for index in range(count)]
    top = functools.reduce(jnp.maximum, parts)
    parts = [jnp.exp(part - top) for part in parts]
    total = functools.reduce(jnp.add, parts)
    weights = jnp.concatenate([part / total for part in parts], axis=0).astype(jnp.bfloat16)
    weights = jnp.dot(weights, spread, preferred_element_type=jnp.float32)
    mixed = functools.reduce(
        jnp.add,
        [
            weights[index * pitch : (index + 1) * pitch]
            * value_stage[pl.ds(index * pitch, pitch), :]
            for index in range(count)
        ],
    )
    out[0] = mixed[:rows].astype(jnp.bfloat16)


def mix(arrived, w_query, w_key, w_value):
    _, rows, width = arrived[0].shape
    pitch = ceil_to(rows, 8)
    count = sum(array.shape[0] for array in arrived)
    total = ceil_to(count * pitch, 16)
    return pl.pallas_call(
        functools.partial(mix_kernel, width // HEADS, len(arrived)),
        out_shape=jax.ShapeDtypeStruct((1, rows, width), jnp.bfloat16),
        in_specs=[VMEM] * (len(arrived) + 3),
        out_specs=VMEM,
        scratch_shapes=[pltpu.VMEM((total, width), jnp.float32)] * 3,
        compiler_params=pltpu.CompilerParams(vmem_limit_bytes=48 << 20),
        cost_estimate=pl.CostEstimate(
            flops=4 * count * rows * width * width, bytes_accessed=4 << 20, transcendentals=0
        ),
        name="mix",
    )(*arrived, w_query, w_key, w_value)


def rounds(total):
    for step in range(1, total):
        if total & (total - 1) == 0:
            there = [(index, index ^ step) for index in range(total)]
        else:
            there = [(index, (index + step) % total) for index in range(total)]
        yield there, [(target, source) for source, target in there]


def chip_rounds(total):
    for there, back in rounds(total // 2):
        yield tuple(
            [(2 * source + core, 2 * target + core) for source, target in pairs for core in range(2)]
            for pairs in (there, back)
        )


def per_device(query_tokens, key_tokens, value_tokens, w_query, w_key, w_value):
    frame_total = lax.axis_size("frame")
    block_total = lax.axis_size("qblk")
    swap = [(index, index ^ 1) for index in range(frame_total)]
    keys, values = [key_tokens], [value_tokens]
    for there, _ in rounds(block_total):
        keys.append(lax.ppermute(key_tokens, "qblk", there))
        values.append(lax.ppermute(value_tokens, "qblk", there))
    paths = list(chip_rounds(frame_total))
    queries = [query_tokens] + [lax.ppermute(query_tokens, "frame", there) for there, _ in paths]
    other_keys = [lax.ppermute(block, "frame", swap) for block in keys]
    other_values = [lax.ppermute(block, "frame", swap) for block in values]
    own = attention(queries, keys, values)
    pooled = attention(queries, other_keys, other_values, own)
    arrived = [pooled[0]] + [
        lax.ppermute(block, "frame", back) for block, (_, back) in zip(pooled[1:], paths)
    ]
    return mix(arrived, w_query, w_key, w_value)


def solution(mesh):
    in_specs = (
        P("frame", "qblk", None),
        P("frame", "qblk", None),
        P("frame", "qblk", None),
        P(),
        P(),
        P(),
    )
    out_specs = P("frame", "qblk", None)
    return jax.shard_map(
        per_device, mesh=mesh, in_specs=in_specs, out_specs=out_specs, check_vma=False
    )
```

```python
import functools
import math

import jax
import jax.numpy as jnp
from jax import lax
from jax.experimental import pallas as pl
from jax.experimental.pallas import tpu as pltpu
from jax.sharding import PartitionSpec as P

HEADS = 12
LANES = 128
VMEM = pl.BlockSpec(memory_space=pltpu.VMEM)
FAR = pl.BlockSpec(memory_space=pltpu.HBM)
NT = (((1,), (1,)), ((), ()))


def far(array):
    return pltpu.with_memory_space_constraint(array, pltpu.HBM)


def ceil_to(value, unit):
    return -(-value // unit) * unit


def stack_rows(blocks, stage):
    rows = blocks[0].shape[0]
    pitch = ceil_to(rows, 8)
    for index, block in enumerate(blocks):
        stage[pl.ds(index * pitch, rows), :] = block.astype(jnp.float32)
        if pitch > rows:
            stage[pl.ds(index * pitch + rows, pitch - rows), :] = jnp.zeros(
                (pitch - rows, stage.shape[1]), jnp.float32
            )
    return stage[...].astype(jnp.bfloat16)


def attend(query, key, value, valid, head_width, put):
    per_slab = LANES // head_width
    factor = math.log2(math.e) / math.sqrt(head_width)
    key_total = key.shape[0]
    lane = lax.broadcasted_iota(jnp.int32, (key_total, LANES), 1) // head_width
    bias = jnp.where(valid, 0.0, -1e30)
    for slab in range(query.shape[1] // LANES):
        cut = slice(slab * LANES, (slab + 1) * LANES)
        query_slab, key_slab, value_slab = query[:, cut], key[:, cut], value[:, cut]
        total = None
        for head in range(per_slab):
            own = lane == head
            masked_key = jnp.where(own, key_slab, 0)
            scores = lax.dot_general(query_slab, masked_key, NT, preferred_element_type=jnp.float32)
            scores = scores + bias
            top = jnp.max(scores, axis=1, keepdims=True)
            weights = jnp.exp2((scores - top) * factor)
            weights = weights * (1.0 / jnp.sum(weights, axis=1, keepdims=True))
            part = jnp.dot(
                weights.astype(jnp.bfloat16),
                jnp.where(own, value_slab, 0),
                preferred_element_type=jnp.float32,
            )
            total = part if total is None else total + part
        put(slab, total)


def pair_kernel(key, value, out, sems):
    copies = [
        pltpu.make_async_copy(ref.at[0], out.at[index], sems.at[index])
        for index, ref in enumerate((key, value))
    ]
    for copy in copies:
        copy.start()
    for copy in copies:
        copy.wait()


def pair(key, value):
    return pl.pallas_call(
        pair_kernel,
        out_shape=pltpu.VMEM((2,) + key.shape[1:], key.dtype),
        in_specs=[FAR] * 2,
        out_specs=VMEM,
        scratch_shapes=[pltpu.SemaphoreType.DMA((2,))],
        name="pair",
    )(far(key), far(value))


def stage_kernel(arrived, *refs):
    queries, own, weights = refs[:arrived], refs[arrived], refs[arrived + 1 : arrived + 4]
    stacked, *held = refs[arrived + 4 : arrived + 8]
    stage, own_block, sems = refs[arrived + 8 :]
    copies = [
        pltpu.make_async_copy(source, target, sems.at[index])
        for index, (source, target) in enumerate(zip((own, *weights), (own_block, *held)))
    ]
    for copy in copies:
        copy.start()
    copies[0].wait()
    stacked[...] = stack_rows([own_block[0]] + [ref[0] for ref in queries], stage)
    for copy in copies[1:]:
        copy.wait()


def stage_operands(arrived, own, weights):
    _, rows, width = own.shape
    total = (len(arrived) + 1) * ceil_to(rows, 8)
    return pl.pallas_call(
        functools.partial(stage_kernel, len(arrived)),
        out_shape=[pltpu.VMEM((total, width), own.dtype)]
        + [pltpu.VMEM(matrix.shape, matrix.dtype) for matrix in weights],
        in_specs=[VMEM] * len(arrived) + [FAR] * 4,
        out_specs=[VMEM] * 4,
        scratch_shapes=[
            pltpu.VMEM((total, width), jnp.float32),
            pltpu.VMEM(own.shape, own.dtype),
            pltpu.SemaphoreType.DMA((4,)),
        ],
        compiler_params=pltpu.CompilerParams(vmem_limit_bytes=32 << 20),
        cost_estimate=pl.CostEstimate(flops=0, bytes_accessed=8 << 20, transcendentals=0),
        name="stage",
    )(*arrived, far(own), *map(far, weights))


def attention_kernel(head_width, query_count, block_count, has_earlier, *refs):
    query, blocks = refs[0], refs[1 : 1 + block_count]
    refs = refs[1 + block_count :]
    earlier = refs[:query_count] if has_earlier else ()
    refs = refs[len(earlier) :]
    outs, (key_stage, value_stage) = refs[:query_count], refs[query_count:]
    rows = blocks[0].shape[-2]
    pitch = ceil_to(rows, 8)
    key = stack_rows([ref[0] for ref in blocks], key_stage)
    value = stack_rows([ref[1] for ref in blocks], value_stage)
    place = lax.broadcasted_iota(jnp.int32, (1, key.shape[0]), 1)
    valid = lax.rem(place, pitch) < rows

    def put(slab, pooled):
        for index, out in enumerate(outs):
            out[out.shape[0] - 1, :, pl.ds(slab * LANES, LANES)] = pooled[
                index * pitch : index * pitch + rows
            ].astype(jnp.bfloat16)

    attend(query[...], key, value, valid, head_width, put)
    for index, ref in enumerate(earlier):
        outs[index][0] = ref[0]


def attention(query, blocks, earlier=()):
    _, rows, width = blocks[0].shape
    pitch = ceil_to(rows, 8)
    count = query.shape[0] // pitch
    kernel = functools.partial(attention_kernel, width // HEADS, count, len(blocks), bool(earlier))
    flops = 4 * count * rows * len(blocks) * rows * width
    shape = jax.ShapeDtypeStruct((2 if earlier else 1, rows, width), jnp.bfloat16)
    return pl.pallas_call(
        kernel,
        out_shape=[shape] * count,
        in_specs=[VMEM] * (1 + len(blocks) + len(earlier)),
        out_specs=[VMEM] * count,
        scratch_shapes=[pltpu.VMEM((len(blocks) * pitch, width), jnp.float32)] * 2,
        compiler_params=pltpu.CompilerParams(vmem_limit_bytes=32 << 20),
        cost_estimate=pl.CostEstimate(flops=flops, bytes_accessed=1 << 20, transcendentals=0),
        name="attention",
    )(query, *blocks, *earlier)


def mix_kernel(head_width, pieces, *refs):
    arrived = refs[:pieces]
    w_query, w_key, w_value, out, stage, key_stage, value_stage = refs[pieces:]
    blocks = [ref[index] for ref in arrived for index in range(ref.shape[0])]
    rows, width = blocks[0].shape
    pitch = ceil_to(rows, 8)
    count = len(blocks)
    scale = 1.0 / math.sqrt(head_width)
    pooled = stack_rows(blocks, stage)
    own = pooled[:ceil_to(rows, 16)]
    query = jnp.dot(own, w_query[...], preferred_element_type=jnp.float32)[:pitch]
    query = query.astype(jnp.bfloat16).astype(jnp.float32)
    key_stage[...] = (
        jnp.dot(pooled, w_key[...], preferred_element_type=jnp.float32)
        .astype(jnp.bfloat16)
        .astype(jnp.float32)
    )
    value_stage[...] = (
        jnp.dot(pooled, w_value[...], preferred_element_type=jnp.float32)
        .astype(jnp.bfloat16)
        .astype(jnp.float32)
    )
    member = (
        lax.broadcasted_iota(jnp.int32, (width, LANES), 0) // head_width
        == lax.broadcasted_iota(jnp.int32, (width, LANES), 1)
    ).astype(jnp.bfloat16)
    spread = (
        lax.broadcasted_iota(jnp.int32, (LANES, width), 1) // head_width
        == lax.broadcasted_iota(jnp.int32, (LANES, width), 0)
    ).astype(jnp.bfloat16)
    product = jnp.concatenate(
        [key_stage[pl.ds(index * pitch, pitch), :] * query for index in range(count)], axis=0
    )
    high = product.astype(jnp.bfloat16)
    low = (product - high.astype(jnp.float32)).astype(jnp.bfloat16)
    scores = jnp.dot(high, member, preferred_element_type=jnp.float32) + jnp.dot(
        low, member, preferred_element_type=jnp.float32
    )
    scores = scores * scale
    parts = [scores[index * pitch : (index + 1) * pitch] for index in range(count)]
    top = functools.reduce(jnp.maximum, parts)
    parts = [jnp.exp(part - top) for part in parts]
    total = functools.reduce(jnp.add, parts)
    weights = jnp.concatenate([part / total for part in parts], axis=0).astype(jnp.bfloat16)
    weights = jnp.dot(weights, spread, preferred_element_type=jnp.float32)
    mixed = functools.reduce(
        jnp.add,
        [
            weights[index * pitch : (index + 1) * pitch]
            * value_stage[pl.ds(index * pitch, pitch), :]
            for index in range(count)
        ],
    )
    out[0] = mixed[:rows].astype(jnp.bfloat16)


def mix(arrived, w_query, w_key, w_value):
    _, rows, width = arrived[0].shape
    pitch = ceil_to(rows, 8)
    count = sum(array.shape[0] for array in arrived)
    total = ceil_to(count * pitch, 16)
    return pl.pallas_call(
        functools.partial(mix_kernel, width // HEADS, len(arrived)),
        out_shape=jax.ShapeDtypeStruct((1, rows, width), jnp.bfloat16),
        in_specs=[VMEM] * (len(arrived) + 3),
        out_specs=VMEM,
        scratch_shapes=[pltpu.VMEM((total, width), jnp.float32)] * 3,
        compiler_params=pltpu.CompilerParams(vmem_limit_bytes=32 << 20),
        cost_estimate=pl.CostEstimate(
            flops=4 * count * rows * width * width, bytes_accessed=4 << 20, transcendentals=0
        ),
        name="mix",
    )(*arrived, w_query, w_key, w_value)


def rounds(total):
    for step in range(1, total):
        if total & (total - 1) == 0:
            there = [(index, index ^ step) for index in range(total)]
        else:
            there = [(index, (index + step) % total) for index in range(total)]
        yield there, [(target, source) for source, target in there]


def chip_rounds(total):
    for there, back in rounds(total // 2):
        yield tuple(
            [(2 * source + core, 2 * target + core) for source, target in pairs for core in range(2)]
            for pairs in (there, back)
        )


def per_device(query_tokens, key_tokens, value_tokens, w_query, w_key, w_value):
    frame_total = lax.axis_size("frame")
    block_total = lax.axis_size("qblk")
    swap = [(index, index ^ 1) for index in range(frame_total)]
    own_block = pair(key_tokens, value_tokens)
    blocks = [own_block] + [lax.ppermute(own_block, "qblk", there) for there, _ in rounds(block_total)]
    paths = list(chip_rounds(frame_total))
    queries = [lax.ppermute(query_tokens, "frame", there) for there, _ in paths]
    query, *weights = stage_operands(queries, query_tokens, (w_query, w_key, w_value))
    held = lax.optimization_barrier((query, *blocks))
    query, blocks = held[0], held[1:]
    other_blocks = [lax.ppermute(block, "frame", swap) for block in blocks]
    own = attention(query, blocks)
    pooled = attention(query, other_blocks, own)
    arrived = [pooled[0]] + [
        lax.ppermute(block, "frame", back) for block, (_, back) in zip(pooled[1:], paths)
    ]
    return mix(arrived, *weights)


def solution(mesh):
    in_specs = (
        P("frame", "qblk", None),
        P("frame", "qblk", None),
        P("frame", "qblk", None),
        P(),
        P(),
        P(),
    )
    out_specs = P("frame", "qblk", None)
    return jax.shard_map(
        per_device, mesh=mesh, in_specs=in_specs, out_specs=out_specs, check_vma=False
    )
```

```python
import functools
import math

import jax
import jax.numpy as jnp
from jax import lax
from jax.experimental import pallas as pl
from jax.experimental.pallas import tpu as pltpu
from jax.sharding import PartitionSpec as P

HEADS = 12
LANES = 128
VMEM = pl.BlockSpec(memory_space=pltpu.VMEM)
FAR = pl.BlockSpec(memory_space=pltpu.HBM)
NT = (((1,), (1,)), ((), ()))


def far(array):
    return pltpu.with_memory_space_constraint(array, pltpu.HBM)


def ceil_to(value, unit):
    return -(-value // unit) * unit


def stack_rows(blocks, stage):
    rows = blocks[0].shape[0]
    pitch = ceil_to(rows, 8)
    for index, block in enumerate(blocks):
        stage[pl.ds(index * pitch, rows), :] = block.astype(jnp.float32)
        if pitch > rows:
            stage[pl.ds(index * pitch + rows, pitch - rows), :] = jnp.zeros(
                (pitch - rows, stage.shape[1]), jnp.float32
            )
    return stage[...].astype(jnp.bfloat16)


def attend(query, key, value, valid, head_width, put):
    per_slab = LANES // head_width
    factor = math.log2(math.e) / math.sqrt(head_width)
    key_total = key.shape[0]
    lane = lax.broadcasted_iota(jnp.int32, (key_total, LANES), 1) // head_width
    bias = jnp.where(valid, 0.0, -1e30)
    for slab in range(query.shape[1] // LANES):
        cut = slice(slab * LANES, (slab + 1) * LANES)
        query_slab, key_slab, value_slab = query[:, cut], key[:, cut], value[:, cut]
        total = None
        for head in range(per_slab):
            own = lane == head
            masked_key = jnp.where(own, key_slab, 0)
            scores = lax.dot_general(query_slab, masked_key, NT, preferred_element_type=jnp.float32)
            scores = scores + bias
            top = jnp.max(scores, axis=1, keepdims=True)
            weights = jnp.exp2((scores - top) * factor)
            weights = weights * (1.0 / jnp.sum(weights, axis=1, keepdims=True))
            part = jnp.dot(
                weights.astype(jnp.bfloat16),
                jnp.where(own, value_slab, 0),
                preferred_element_type=jnp.float32,
            )
            total = part if total is None else total + part
        put(slab, total)


def load_kernel(key, value, query, pair, near_query, sems):
    targets = (pair.at[0], pair.at[1], near_query.at[0])
    copies = [
        pltpu.make_async_copy(source.at[0], target, sems.at[index])
        for index, (source, target) in enumerate(zip((key, value, query), targets))
    ]
    for copy in copies:
        copy.start()
    for copy in copies:
        copy.wait()


def load(key, value, query):
    return pl.pallas_call(
        load_kernel,
        out_shape=[
            pltpu.VMEM((2,) + key.shape[1:], key.dtype),
            pltpu.VMEM(query.shape, query.dtype),
        ],
        in_specs=[FAR] * 3,
        out_specs=[VMEM] * 2,
        scratch_shapes=[pltpu.SemaphoreType.DMA((3,))],
        name="load",
    )(far(key), far(value), far(query))


def fetch_kernel(*refs):
    count = len(refs) // 2
    far_refs, held, sems = refs[:count], refs[count : 2 * count], refs[-1]
    copies = [
        pltpu.make_async_copy(source, target, sems.at[index])
        for index, (source, target) in enumerate(zip(far_refs, held))
    ]
    for copy in copies:
        copy.start()
    for copy in copies:
        copy.wait()


def fetch(weights):
    return pl.pallas_call(
        fetch_kernel,
        out_shape=[pltpu.VMEM(matrix.shape, matrix.dtype) for matrix in weights],
        in_specs=[FAR] * len(weights),
        out_specs=[VMEM] * len(weights),
        scratch_shapes=[pltpu.SemaphoreType.DMA((len(weights),))],
        compiler_params=pltpu.CompilerParams(vmem_limit_bytes=32 << 20),
        cost_estimate=pl.CostEstimate(flops=0, bytes_accessed=len(weights) << 21, transcendentals=0),
        name="fetch",
    )(*map(far, weights))


def attention_kernel(head_width, query_count, forms, *refs):
    first = query_count > 1
    queries, refs = refs[:query_count], refs[query_count:]
    keys, values = [], []
    for form in forms:
        keys.append(refs[0].at[0])
        values.append(refs[form - 1].at[2 - form])
        refs = refs[form:]
    if first:
        *outs, stacked, key_stage, value_stage, query_stage = refs
        query = stack_rows([ref[0] for ref in queries], query_stage)
        stacked[...] = query
        earlier = ()
    else:
        *refs, key_stage, value_stage = refs
        earlier, outs = refs[: len(refs) // 2], refs[len(refs) // 2 :]
        query = queries[0][...]
    rows = keys[0].shape[-2]
    pitch = ceil_to(rows, 8)
    key = stack_rows([ref[...] for ref in keys], key_stage)
    value = stack_rows([ref[...] for ref in values], value_stage)
    place = lax.broadcasted_iota(jnp.int32, (1, key.shape[0]), 1)
    valid = lax.rem(place, pitch) < rows

    def put(slab, pooled):
        for index, out in enumerate(outs):
            out[out.shape[0] - 1, :, pl.ds(slab * LANES, LANES)] = pooled[
                index * pitch : index * pitch + rows
            ].astype(jnp.bfloat16)

    attend(query, key, value, valid, head_width, put)
    for out, ref in zip(outs, earlier):
        out[0] = ref[0]


def attention(queries, blocks, earlier=()):
    _, rows, width = blocks[0][0].shape
    pitch = ceil_to(rows, 8)
    count = len(earlier) or len(queries)
    total = count * pitch
    flops = 4 * count * rows * len(blocks) * rows * width
    shape = jax.ShapeDtypeStruct((2 if earlier else 1, rows, width), jnp.bfloat16)
    first = not earlier
    out = pl.pallas_call(
        functools.partial(attention_kernel, width // HEADS, len(queries), [len(block) for block in blocks]),
        out_shape=[shape] * count + [near((total, width), jnp.bfloat16)] * first,
        in_specs=[VMEM] * (len(queries) + sum(map(len, blocks)) + len(earlier)),
        out_specs=[VMEM] * (count + first),
        scratch_shapes=[near((len(blocks) * pitch, width))] * 2 + [near((total, width))] * first,
        compiler_params=pltpu.CompilerParams(vmem_limit_bytes=32 << 20),
        cost_estimate=pl.CostEstimate(flops=flops, bytes_accessed=1 << 20, transcendentals=0),
        name="attention",
    )(*queries, *(array for block in blocks for array in block), *earlier)
    return out


def head_members(width, head_width):
    channel = lax.broadcasted_iota(jnp.int32, (width, LANES), 0) // head_width
    return (channel == lax.broadcasted_iota(jnp.int32, (width, LANES), 1)).astype(jnp.bfloat16)


def head_spread(width, head_width):
    channel = lax.broadcasted_iota(jnp.int32, (LANES, width), 1) // head_width
    return (channel == lax.broadcasted_iota(jnp.int32, (LANES, width), 0)).astype(jnp.bfloat16)


def project(rows, matrix):
    wide = jnp.dot(rows, matrix[...], preferred_element_type=jnp.float32)
    return wide.astype(jnp.bfloat16).astype(jnp.float32)


def score(query, pooled, w_key, head_width):
    path_key = project(pooled, w_key)
    pitch, width = query.shape
    product = jnp.concatenate(
        [path_key[at : at + pitch] * query for at in range(0, path_key.shape[0], pitch)], axis=0
    )
    member = head_members(width, head_width)
    high = product.astype(jnp.bfloat16)
    low = (product - high.astype(jnp.float32)).astype(jnp.bfloat16)
    scores = jnp.dot(high, member, preferred_element_type=jnp.float32) + jnp.dot(
        low, member, preferred_element_type=jnp.float32
    )
    return scores * (1.0 / math.sqrt(head_width))


def stack_pooled(ref, stage):
    return stack_rows([ref[index] for index in range(ref.shape[0])], stage)


def own_kernel(head_width, block, w_query, w_key, w_value, query, scores, values, stage):
    pooled = stack_pooled(block, stage)
    rows, pitch = block.shape[1], query.shape[0]
    query[...] = project(pooled[: ceil_to(rows, 16)], w_query)[:pitch]
    scores[...] = score(query[...], pooled, w_key, head_width)
    values[...] = project(pooled, w_value)


def part_kernel(head_width, block, query, w_key, w_value, scores, values, stage):
    pooled = stack_pooled(block, stage)
    scores[...] = score(query[...], pooled, w_key, head_width)
    values[...] = project(pooled, w_value)


def last_kernel(head_width, earlier, count, *refs):
    blocks, (query, w_key, w_value), refs = refs[:count], refs[count : count + 3], refs[count + 3 :]
    score_refs, value_refs, (out, stage) = refs[:earlier], refs[earlier : 2 * earlier], refs[-2:]
    pooled = stack_rows([ref[index] for ref in blocks for index in range(ref.shape[0])], stage)
    pitch, width = query.shape
    score_parts = [ref[...] for ref in score_refs] + [score(query[...], pooled, w_key, head_width)]
    value_parts = [ref[...] for ref in value_refs] + [project(pooled, w_value)]
    places = [
        (part, at) for part in range(earlier + 1) for at in range(0, score_parts[part].shape[0], pitch)
    ]
    scores = [score_parts[part][at : at + pitch] for part, at in places]
    top = functools.reduce(jnp.maximum, scores)
    scores = [jnp.exp(part - top) for part in scores]
    share = 1.0 / functools.reduce(jnp.add, scores)
    weights = jnp.concatenate([part * share for part in scores], axis=0).astype(jnp.bfloat16)
    weights = jnp.dot(weights, head_spread(width, head_width), preferred_element_type=jnp.float32)
    mixed = functools.reduce(
        jnp.add,
        [
            weights[index * pitch : (index + 1) * pitch] * value_parts[part][at : at + pitch]
            for index, (part, at) in enumerate(places)
        ],
    )
    out[0] = mixed[: blocks[0].shape[1]].astype(jnp.bfloat16)


def near(shape, dtype=jnp.float32):
    return pltpu.VMEM(shape, dtype)


def mix_call(kernel, blocks, out_shape, operands, name):
    _, rows, width = blocks[0].shape
    count = sum(block.shape[0] for block in blocks)
    return pl.pallas_call(
        functools.partial(kernel, width // HEADS),
        out_shape=out_shape,
        in_specs=[VMEM] * (len(blocks) + len(operands)),
        out_specs=jax.tree.map(lambda _: VMEM, out_shape),
        scratch_shapes=[near((count * ceil_to(rows, 8), width))],
        compiler_params=pltpu.CompilerParams(vmem_limit_bytes=32 << 20),
        cost_estimate=pl.CostEstimate(
            flops=4 * count * rows * width * width, bytes_accessed=4 << 20, transcendentals=0
        ),
        name=name,
    )(*blocks, *operands)


def part_shapes(block):
    count, rows, width = block.shape
    total = count * ceil_to(rows, 8)
    return [near((total, LANES)), near((total, width))]


def mix_own(block, weights):
    _, rows, width = block.shape
    shapes = [near((ceil_to(rows, 8), width)), *part_shapes(block)]
    query, *part = mix_call(own_kernel, [block], shapes, weights, "mix_own")
    return query, tuple(part)


def mix_part(block, query, w_key, w_value):
    return mix_call(part_kernel, [block], part_shapes(block), (query, w_key, w_value), "mix_part")


def mix_last(blocks, query, w_key, w_value, parts):
    scores, values = zip(*parts)
    return mix_call(
        lambda head_width, *refs: last_kernel(head_width, len(parts), len(blocks), *refs),
        blocks,
        jax.ShapeDtypeStruct((1,) + blocks[0].shape[1:], blocks[0].dtype),
        (query, w_key, w_value, *scores, *values),
        "mix_last",
    )


def rounds(total):
    for step in range(1, total):
        if total & (total - 1) == 0:
            there = [(index, index ^ step) for index in range(total)]
        else:
            there = [(index, (index + step) % total) for index in range(total)]
        yield there, [(target, source) for source, target in there]


def chip_rounds(total):
    for there, back in rounds(total // 2):
        yield tuple(
            [(2 * source + core, 2 * target + core) for source, target in pairs for core in range(2)]
            for pairs in (there, back)
        )


def per_device(query_tokens, key_tokens, value_tokens, w_query, w_key, w_value):
    frame_total = lax.axis_size("frame")
    block_total = lax.axis_size("qblk")
    swap = [(index, index ^ 1) for index in range(frame_total)]
    own_block, near_query = load(key_tokens, value_tokens, query_tokens)
    blocks = [(own_block,)] + [(lax.ppermute(own_block, "qblk", there),) for there, _ in rounds(block_total)]
    paths = list(chip_rounds(frame_total))
    ready_query = lax.optimization_barrier((near_query, blocks[1 % len(blocks)][0]))[0]
    queries = [near_query] + [lax.ppermute(ready_query, "frame", there) for there, _ in paths]
    w_query, w_key, w_value = fetch((w_query, w_key, w_value))
    *queries, w_query, w_key, w_value = lax.optimization_barrier((*queries, w_query, w_key, w_value))
    turned = [lax.optimization_barrier((blocks[0], blocks[1 % len(blocks)]))[0], *blocks[1:2]]
    turned += [lax.optimization_barrier((block, *queries))[0] for block in blocks[2:]]
    other_blocks = [
        tuple(lax.ppermute(array, "frame", swap) for array in block) for block in turned
    ]
    *own, query = attention(queries, blocks)
    pooled = attention([query], other_blocks, own)
    own_query, part = mix_own(pooled[0], (w_query, w_key, w_value))
    if not paths:
        return mix_last([pooled[0]], own_query, w_key, w_value, [])
    *nearer, own_query = lax.optimization_barrier((*pooled[1:-1], own_query))
    arrived = [
        lax.ppermute(block, "frame", back)
        for block, (_, back) in zip([*nearer, pooled[-1]], paths)
    ]
    parts = [part]
    for block in arrived[:1:-1]:
        parts.append(mix_part(block, own_query, w_key, w_value))
    return mix_last(arrived[:2], own_query, w_key, w_value, parts)


def solution(mesh):
    in_specs = (
        P("frame", "qblk", None),
        P("frame", "qblk", None),
        P("frame", "qblk", None),
        P(),
        P(),
        P(),
    )
    out_specs = P("frame", "qblk", None)
    return jax.shard_map(
        per_device, mesh=mesh, in_specs=in_specs, out_specs=out_specs, check_vma=False
    )
```

```python
import functools
import math

import jax
import jax.numpy as jnp
from jax import lax
from jax.experimental import pallas as pl
from jax.experimental.pallas import tpu as pltpu
from jax.sharding import PartitionSpec as P

HEADS = 12
LANES = 128
VMEM = pl.BlockSpec(memory_space=pltpu.VMEM)
FAR = pl.BlockSpec(memory_space=pltpu.HBM)
NT = (((1,), (1,)), ((), ()))


def far(array):
    return pltpu.with_memory_space_constraint(array, pltpu.HBM)


def ceil_to(value, unit):
    return -(-value // unit) * unit


def stack_rows(blocks, stage):
    rows = blocks[0].shape[0]
    pitch = ceil_to(rows, 8)
    for index, block in enumerate(blocks):
        stage[pl.ds(index * pitch, rows), :] = block.astype(jnp.float32)
        if pitch > rows:
            stage[pl.ds(index * pitch + rows, pitch - rows), :] = jnp.zeros(
                (pitch - rows, stage.shape[1]), jnp.float32
            )
    return stage[...].astype(jnp.bfloat16)


def attend(query, key, value, valid, head_width, put):
    per_slab = LANES // head_width
    factor = math.log2(math.e) / math.sqrt(head_width)
    key_total = key.shape[0]
    lane = lax.broadcasted_iota(jnp.int32, (key_total, LANES), 1) // head_width
    bias = jnp.where(valid, 0.0, -1e30)
    for slab in range(query.shape[1] // LANES):
        cut = slice(slab * LANES, (slab + 1) * LANES)
        query_slab, key_slab, value_slab = query[:, cut], key[:, cut], value[:, cut]
        total = None
        for head in range(per_slab):
            own = lane == head
            masked_key = jnp.where(own, key_slab, 0)
            scores = lax.dot_general(query_slab, masked_key, NT, preferred_element_type=jnp.float32)
            scores = scores + bias
            top = jnp.max(scores, axis=1, keepdims=True)
            weights = jnp.exp2((scores - top) * factor)
            weights = weights * (1.0 / jnp.sum(weights, axis=1, keepdims=True))
            part = jnp.dot(
                weights.astype(jnp.bfloat16),
                jnp.where(own, value_slab, 0),
                preferred_element_type=jnp.float32,
            )
            total = part if total is None else total + part
        put(slab, total)


def load_kernel(key, value, query, pair, near_query, sems):
    targets = (pair.at[0], pair.at[1], near_query.at[0])
    copies = [
        pltpu.make_async_copy(source.at[0], target, sems.at[index])
        for index, (source, target) in enumerate(zip((key, value, query), targets))
    ]
    for copy in copies:
        copy.start()
    for copy in copies:
        copy.wait()


def load(key, value, query):
    return pl.pallas_call(
        load_kernel,
        out_shape=[
            pltpu.VMEM((2,) + key.shape[1:], key.dtype),
            pltpu.VMEM(query.shape, query.dtype),
        ],
        in_specs=[FAR] * 3,
        out_specs=[VMEM] * 2,
        scratch_shapes=[pltpu.SemaphoreType.DMA((3,))],
        name="load",
    )(far(key), far(value), far(query))


def fetch_kernel(*refs):
    count = len(refs) // 2
    far_refs, held, sems = refs[:count], refs[count : 2 * count], refs[-1]
    copies = [
        pltpu.make_async_copy(source, target, sems.at[index])
        for index, (source, target) in enumerate(zip(far_refs, held))
    ]
    for copy in copies:
        copy.start()
    for copy in copies:
        copy.wait()


def fetch(weights):
    return pl.pallas_call(
        fetch_kernel,
        out_shape=[pltpu.VMEM(matrix.shape, matrix.dtype) for matrix in weights],
        in_specs=[FAR] * len(weights),
        out_specs=[VMEM] * len(weights),
        scratch_shapes=[pltpu.SemaphoreType.DMA((len(weights),))],
        compiler_params=pltpu.CompilerParams(vmem_limit_bytes=32 << 20),
        cost_estimate=pl.CostEstimate(flops=0, bytes_accessed=len(weights) << 21, transcendentals=0),
        name="fetch",
    )(*map(far, weights))


def attention_kernel(head_width, query_count, forms, *refs):
    first = query_count > 1
    queries, refs = refs[:query_count], refs[query_count:]
    keys, values = [], []
    for form in forms:
        keys.append(refs[0].at[0])
        values.append(refs[form - 1].at[2 - form])
        refs = refs[form:]
    if first:
        *outs, stacked, key_stage, value_stage, query_stage = refs
        query = stack_rows([ref[0] for ref in queries], query_stage)
        stacked[...] = query
        earlier = ()
    else:
        *refs, key_stage, value_stage = refs
        earlier, outs = refs[: len(refs) // 2], refs[len(refs) // 2 :]
        query = queries[0][...]
    rows = keys[0].shape[-2]
    pitch = ceil_to(rows, 8)
    key = stack_rows([ref[...] for ref in keys], key_stage)
    value = stack_rows([ref[...] for ref in values], value_stage)
    place = lax.broadcasted_iota(jnp.int32, (1, key.shape[0]), 1)
    valid = lax.rem(place, pitch) < rows

    def put(slab, pooled):
        for index, out in enumerate(outs):
            out[out.shape[0] - 1, :, pl.ds(slab * LANES, LANES)] = pooled[
                index * pitch : index * pitch + rows
            ].astype(jnp.bfloat16)

    attend(query, key, value, valid, head_width, put)
    for out, ref in zip(outs, earlier):
        out[0] = ref[0]


def attention(queries, blocks, earlier=()):
    _, rows, width = blocks[0][0].shape
    pitch = ceil_to(rows, 8)
    count = len(earlier) or len(queries)
    total = count * pitch
    flops = 4 * count * rows * len(blocks) * rows * width
    shape = jax.ShapeDtypeStruct((2 if earlier else 1, rows, width), jnp.bfloat16)
    first = not earlier
    out = pl.pallas_call(
        functools.partial(attention_kernel, width // HEADS, len(queries), [len(block) for block in blocks]),
        out_shape=[shape] * count + [near((total, width), jnp.bfloat16)] * first,
        in_specs=[VMEM] * (len(queries) + sum(map(len, blocks)) + len(earlier)),
        out_specs=[VMEM] * (count + first),
        scratch_shapes=[near((len(blocks) * pitch, width))] * 2 + [near((total, width))] * first,
        compiler_params=pltpu.CompilerParams(vmem_limit_bytes=32 << 20),
        cost_estimate=pl.CostEstimate(flops=flops, bytes_accessed=1 << 20, transcendentals=0),
        name="attention",
    )(*queries, *(array for block in blocks for array in block), *earlier)
    return out


def head_members(width, head_width):
    channel = lax.broadcasted_iota(jnp.int32, (width, LANES), 0) // head_width
    return (channel == lax.broadcasted_iota(jnp.int32, (width, LANES), 1)).astype(jnp.bfloat16)


def head_spread(width, head_width):
    channel = lax.broadcasted_iota(jnp.int32, (LANES, width), 1) // head_width
    return (channel == lax.broadcasted_iota(jnp.int32, (LANES, width), 0)).astype(jnp.bfloat16)


def project(rows, matrix):
    wide = jnp.dot(rows, matrix[...], preferred_element_type=jnp.float32)
    return wide.astype(jnp.bfloat16).astype(jnp.float32)


def score(query, pooled, w_key, head_width):
    path_key = project(pooled, w_key)
    pitch, width = query.shape
    product = jnp.concatenate(
        [path_key[at : at + pitch] * query for at in range(0, path_key.shape[0], pitch)], axis=0
    )
    member = head_members(width, head_width)
    high = product.astype(jnp.bfloat16)
    low = (product - high.astype(jnp.float32)).astype(jnp.bfloat16)
    scores = jnp.dot(high, member, preferred_element_type=jnp.float32) + jnp.dot(
        low, member, preferred_element_type=jnp.float32
    )
    return scores * (1.0 / math.sqrt(head_width))


def stack_pooled(ref, stage):
    return stack_rows([ref[index] for index in range(ref.shape[0])], stage)


def own_kernel(head_width, block, w_query, w_key, w_value, query, scores, values, stage):
    pooled = stack_pooled(block, stage)
    rows, pitch = block.shape[1], query.shape[0]
    query[...] = project(pooled[: ceil_to(rows, 16)], w_query)[:pitch]
    scores[...] = score(query[...], pooled, w_key, head_width)
    values[...] = project(pooled, w_value)


def part_kernel(head_width, block, query, w_key, w_value, scores, values, stage):
    pooled = stack_pooled(block, stage)
    scores[...] = score(query[...], pooled, w_key, head_width)
    values[...] = project(pooled, w_value)


def last_kernel(head_width, earlier, count, *refs):
    blocks, (query, w_key, w_value), refs = refs[:count], refs[count : count + 3], refs[count + 3 :]
    score_refs, value_refs, (out, stage) = refs[:earlier], refs[earlier : 2 * earlier], refs[-2:]
    pooled = stack_rows([ref[index] for ref in blocks for index in range(ref.shape[0])], stage)
    pitch, width = query.shape
    score_parts = [ref[...] for ref in score_refs] + [score(query[...], pooled, w_key, head_width)]
    value_parts = [ref[...] for ref in value_refs] + [project(pooled, w_value)]
    places = [
        (part, at) for part in range(earlier + 1) for at in range(0, score_parts[part].shape[0], pitch)
    ]
    scores = [score_parts[part][at : at + pitch] for part, at in places]
    top = functools.reduce(jnp.maximum, scores)
    scores = [jnp.exp(part - top) for part in scores]
    share = 1.0 / functools.reduce(jnp.add, scores)
    weights = jnp.concatenate([part * share for part in scores], axis=0).astype(jnp.bfloat16)
    weights = jnp.dot(weights, head_spread(width, head_width), preferred_element_type=jnp.float32)
    mixed = functools.reduce(
        jnp.add,
        [
            weights[index * pitch : (index + 1) * pitch] * value_parts[part][at : at + pitch]
            for index, (part, at) in enumerate(places)
        ],
    )
    out[0] = mixed[: blocks[0].shape[1]].astype(jnp.bfloat16)


def near(shape, dtype=jnp.float32):
    return pltpu.VMEM(shape, dtype)


def mix_call(kernel, blocks, out_shape, operands, name):
    _, rows, width = blocks[0].shape
    count = sum(block.shape[0] for block in blocks)
    return pl.pallas_call(
        functools.partial(kernel, width // HEADS),
        out_shape=out_shape,
        in_specs=[VMEM] * (len(blocks) + len(operands)),
        out_specs=jax.tree.map(lambda _: VMEM, out_shape),
        scratch_shapes=[near((count * ceil_to(rows, 8), width))],
        compiler_params=pltpu.CompilerParams(vmem_limit_bytes=32 << 20),
        cost_estimate=pl.CostEstimate(
            flops=4 * count * rows * width * width, bytes_accessed=4 << 20, transcendentals=0
        ),
        name=name,
    )(*blocks, *operands)


def part_shapes(block):
    count, rows, width = block.shape
    total = count * ceil_to(rows, 8)
    return [near((total, LANES)), near((total, width))]


def mix_own(block, weights):
    _, rows, width = block.shape
    shapes = [near((ceil_to(rows, 8), width)), *part_shapes(block)]
    query, *part = mix_call(own_kernel, [block], shapes, weights, "mix_own")
    return query, tuple(part)


def mix_part(block, query, w_key, w_value):
    return mix_call(part_kernel, [block], part_shapes(block), (query, w_key, w_value), "mix_part")


def mix_last(blocks, query, w_key, w_value, parts):
    scores, values = zip(*parts)
    return mix_call(
        lambda head_width, *refs: last_kernel(head_width, len(parts), len(blocks), *refs),
        blocks,
        jax.ShapeDtypeStruct((1,) + blocks[0].shape[1:], blocks[0].dtype),
        (query, w_key, w_value, *scores, *values),
        "mix_last",
    )


def rounds(total):
    for step in range(1, total):
        if total & (total - 1) == 0:
            there = [(index, index ^ step) for index in range(total)]
        else:
            there = [(index, (index + step) % total) for index in range(total)]
        yield there, [(target, source) for source, target in there]


def chip_rounds(total):
    for there, back in rounds(total // 2):
        yield tuple(
            [(2 * source + core, 2 * target + core) for source, target in pairs for core in range(2)]
            for pairs in (there, back)
        )


def per_device(query_tokens, key_tokens, value_tokens, w_query, w_key, w_value):
    frame_total = lax.axis_size("frame")
    block_total = lax.axis_size("qblk")
    swap = [(index, index ^ 1) for index in range(frame_total)]
    own_block, near_query = load(key_tokens, value_tokens, query_tokens)
    blocks = [(own_block,)] + [(lax.ppermute(own_block, "qblk", there),) for there, _ in rounds(block_total)]
    paths = list(chip_rounds(frame_total))
    ready_query = lax.optimization_barrier((near_query, blocks[1 % len(blocks)][0]))[0]
    queries = [near_query] + [
        lax.ppermute(ready_query if step == 0 else near_query, "frame", there)
        for step, (there, _) in enumerate(paths)
    ]
    w_query, w_key, w_value = fetch((w_query, w_key, w_value))
    *queries, w_query, w_key, w_value = lax.optimization_barrier((*queries, w_query, w_key, w_value))
    turned = [lax.optimization_barrier((block, *queries))[0] for block in blocks]
    other_blocks = [
        tuple(lax.ppermute(array, "frame", swap) for array in block) for block in turned
    ]
    *own, query = attention(queries, blocks)
    pooled = attention([query], other_blocks, own)
    own_query, part = mix_own(pooled[0], (w_query, w_key, w_value))
    if not paths:
        return mix_last([pooled[0]], own_query, w_key, w_value, [])
    arrived = [
        lax.ppermute(block, "frame", back)
        for block, (_, back) in zip(pooled[1:], paths)
    ]
    parts = [part]
    for block in arrived[:1:-1]:
        parts.append(mix_part(block, own_query, w_key, w_value))
    return mix_last(arrived[:2], own_query, w_key, w_value, parts)


def solution(mesh):
    in_specs = (
        P("frame", "qblk", None),
        P("frame", "qblk", None),
        P("frame", "qblk", None),
        P(),
        P(),
        P(),
    )
    out_specs = P("frame", "qblk", None)
    return jax.shard_map(
        per_device, mesh=mesh, in_specs=in_specs, out_specs=out_specs, check_vma=False
    )
```

```python
import functools
import math

import jax
import jax.numpy as jnp
from jax import lax
from jax.experimental import pallas as pl
from jax.experimental.pallas import tpu as pltpu
from jax.sharding import PartitionSpec as P

HEADS = 12
LANES = 128
VMEM = pl.BlockSpec(memory_space=pltpu.VMEM)
FAR = pl.BlockSpec(memory_space=pltpu.HBM)
NT = (((1,), (1,)), ((), ()))
TN = (((0,), (0,)), ((), ()))


def far(array):
    return pltpu.with_memory_space_constraint(array, pltpu.HBM)


def ceil_to(value, unit):
    return -(-value // unit) * unit


def stack_rows(blocks, stage, pitch):
    rows = blocks[0].shape[0]
    for index, block in enumerate(blocks):
        stage[pl.ds(index * pitch, rows), :] = block.astype(jnp.float32)
        end = stage.shape[0] if index == len(blocks) - 1 else (index + 1) * pitch
        gap = end - index * pitch - rows
        if gap:
            stage[pl.ds(index * pitch + rows, gap), :] = jnp.zeros((gap, stage.shape[1]), jnp.float32)
    return stage[...].astype(jnp.bfloat16)


def attend(query, key, value, key_count, head_width, out):
    per_slab = LANES // head_width
    factor = math.log2(math.e) / math.sqrt(head_width)
    query_total, key_total = query.shape[0], key.shape[0]
    head = lax.broadcasted_iota(jnp.int32, (query_total, LANES), 1) // head_width
    for at in range(0, query.shape[1], LANES):
        cut = slice(at, at + LANES)
        side = jnp.concatenate(
            [jnp.where(head == index, query[:, cut], 0) for index in range(per_slab)], axis=0
        )
        scores = lax.dot_general(key[:, cut], side, NT, preferred_element_type=jnp.float32)
        if key_count < key_total:
            place = lax.broadcasted_iota(jnp.int32, (key_total, 1), 0)
            scores = scores + jnp.where(place < key_count, 0.0, -1e30)
        top = jnp.max(scores, axis=0, keepdims=True)
        weights = jnp.exp2((scores - top) * factor)
        weights = weights * (1.0 / jnp.sum(weights, axis=0, keepdims=True))
        pooled = lax.dot_general(
            weights.astype(jnp.bfloat16), value[:, cut], TN, preferred_element_type=jnp.float32
        )
        mine = pooled[:query_total]
        for index in range(1, per_slab):
            mine = jnp.where(head == index, pooled[index * query_total : (index + 1) * query_total], mine)
        out[:, cut] = mine


def load_kernel(key, value, query, pair, near_query, sems):
    targets = (pair.at[0], pair.at[1], near_query.at[0])
    copies = [
        pltpu.make_async_copy(source.at[0], target, sems.at[index])
        for index, (source, target) in enumerate(zip((key, value, query), targets))
    ]
    for copy in copies:
        copy.start()
    for copy in copies:
        copy.wait()


def load(key, value, query):
    return pl.pallas_call(
        load_kernel,
        out_shape=[
            pltpu.VMEM((2,) + key.shape[1:], key.dtype),
            pltpu.VMEM(query.shape, query.dtype),
        ],
        in_specs=[FAR] * 3,
        out_specs=[VMEM] * 2,
        scratch_shapes=[pltpu.SemaphoreType.DMA((3,))],
        name="load",
    )(far(key), far(value), far(query))


def fetch_kernel(*refs):
    count = len(refs) // 2
    far_refs, held, sems = refs[:count], refs[count : 2 * count], refs[-1]
    copies = [
        pltpu.make_async_copy(source, target, sems.at[index])
        for index, (source, target) in enumerate(zip(far_refs, held))
    ]
    for copy in copies:
        copy.start()
    for copy in copies:
        copy.wait()


def fetch(weights):
    return pl.pallas_call(
        fetch_kernel,
        out_shape=[pltpu.VMEM(matrix.shape, matrix.dtype) for matrix in weights],
        in_specs=[FAR] * len(weights),
        out_specs=[VMEM] * len(weights),
        scratch_shapes=[pltpu.SemaphoreType.DMA((len(weights),))],
        compiler_params=pltpu.CompilerParams(vmem_limit_bytes=32 << 20),
        cost_estimate=pl.CostEstimate(flops=0, bytes_accessed=len(weights) << 21, transcendentals=0),
        name="fetch",
    )(*map(far, weights))


def attention_kernel(head_width, query_count, earlier_count, forms, *refs):
    queries, refs = refs[:query_count], refs[query_count:]
    keys, values = [], []
    for form in forms:
        keys.append(refs[0].at[0])
        values.append(refs[form - 1].at[2 - form])
        refs = refs[form:]
    *refs, key_stage, value_stage, query_stage = refs
    rows = keys[0].shape[-2]
    if earlier_count:
        earlier, outs = refs[:earlier_count], refs[earlier_count:]
        query = queries[0][...]
    else:
        earlier, (*outs, stacked) = (), refs
        query = stack_rows([ref[0] for ref in queries], query_stage, rows)
        stacked[...] = query
    key = stack_rows([ref[...] for ref in keys], key_stage, rows)
    value = stack_rows([ref[...] for ref in values], value_stage, rows)
    attend(query, key, value, len(keys) * rows, head_width, query_stage)
    for index, out in enumerate(outs):
        out[out.shape[0] - 1] = query_stage[pl.ds(index * rows, rows), :].astype(out.dtype)
    for out, ref in zip(outs, earlier):
        out[0] = ref[0]


def attention(queries, blocks, earlier=()):
    _, rows, width = blocks[0][0].shape
    count = len(earlier) or len(queries)
    query_total, key_total = ceil_to(count * rows, 16), ceil_to(len(blocks) * rows, 16)
    flops = 4 * count * rows * len(blocks) * rows * width
    shape = jax.ShapeDtypeStruct((2 if earlier else 1, rows, width), jnp.bfloat16)
    first = not earlier
    kernel = functools.partial(
        attention_kernel, width // HEADS, len(queries), len(earlier), [len(block) for block in blocks]
    )
    return pl.pallas_call(
        kernel,
        out_shape=[shape] * count + [near((query_total, width), jnp.bfloat16)] * first,
        in_specs=[VMEM] * (len(queries) + sum(map(len, blocks)) + len(earlier)),
        out_specs=[VMEM] * (count + first),
        scratch_shapes=[near((key_total, width))] * 2 + [near((query_total, width))],
        compiler_params=pltpu.CompilerParams(vmem_limit_bytes=48 << 20),
        cost_estimate=pl.CostEstimate(flops=flops, bytes_accessed=1 << 20, transcendentals=0),
        name="attention",
    )(*queries, *(array for block in blocks for array in block), *earlier)


def head_members(width, head_width):
    channel = lax.broadcasted_iota(jnp.int32, (width, LANES), 0) // head_width
    return (channel == lax.broadcasted_iota(jnp.int32, (width, LANES), 1)).astype(jnp.bfloat16)


def head_spread(width, head_width):
    channel = lax.broadcasted_iota(jnp.int32, (LANES, width), 1) // head_width
    return (channel == lax.broadcasted_iota(jnp.int32, (LANES, width), 0)).astype(jnp.bfloat16)


def project(rows, matrix):
    wide = jnp.dot(rows, matrix[...], preferred_element_type=jnp.float32)
    return wide.astype(jnp.bfloat16).astype(jnp.float32)


def score(query, pooled, w_key, head_width):
    path_key = project(pooled, w_key)
    pitch, width = query.shape
    product = jnp.concatenate(
        [path_key[at : at + pitch] * query for at in range(0, path_key.shape[0], pitch)], axis=0
    )
    member = head_members(width, head_width)
    high = product.astype(jnp.bfloat16)
    low = (product - high.astype(jnp.float32)).astype(jnp.bfloat16)
    scores = jnp.dot(high, member, preferred_element_type=jnp.float32) + jnp.dot(
        low, member, preferred_element_type=jnp.float32
    )
    return scores * (1.0 / math.sqrt(head_width))


def stack_pooled(ref, stage):
    return stack_rows([ref[index] for index in range(ref.shape[0])], stage, ceil_to(ref.shape[1], 8))


def own_kernel(head_width, block, w_query, w_key, w_value, query, scores, values, stage):
    pooled = stack_pooled(block, stage)
    rows, pitch = block.shape[1], query.shape[0]
    query[...] = project(pooled[: ceil_to(rows, 16)], w_query)[:pitch]
    scores[...] = score(query[...], pooled, w_key, head_width)
    values[...] = project(pooled, w_value)


def part_kernel(head_width, block, query, w_key, w_value, scores, values, stage):
    pooled = stack_pooled(block, stage)
    scores[...] = score(query[...], pooled, w_key, head_width)
    values[...] = project(pooled, w_value)


def last_kernel(head_width, earlier, count, *refs):
    blocks, (query, w_key, w_value), refs = refs[:count], refs[count : count + 3], refs[count + 3 :]
    score_refs, value_refs, (out, stage) = refs[:earlier], refs[earlier : 2 * earlier], refs[-2:]
    pitch, width = query.shape
    pooled = stack_rows([ref[index] for ref in blocks for index in range(ref.shape[0])], stage, pitch)
    score_parts = [ref[...] for ref in score_refs] + [score(query[...], pooled, w_key, head_width)]
    value_parts = [ref[...] for ref in value_refs] + [project(pooled, w_value)]
    places = [
        (part, at) for part in range(earlier + 1) for at in range(0, score_parts[part].shape[0], pitch)
    ]
    scores = [score_parts[part][at : at + pitch] for part, at in places]
    top = functools.reduce(jnp.maximum, scores)
    scores = [jnp.exp(part - top) for part in scores]
    share = 1.0 / functools.reduce(jnp.add, scores)
    weights = jnp.concatenate([part * share for part in scores], axis=0).astype(jnp.bfloat16)
    weights = jnp.dot(weights, head_spread(width, head_width), preferred_element_type=jnp.float32)
    mixed = functools.reduce(
        jnp.add,
        [
            weights[index * pitch : (index + 1) * pitch] * value_parts[part][at : at + pitch]
            for index, (part, at) in enumerate(places)
        ],
    )
    out[0] = mixed[: blocks[0].shape[1]].astype(jnp.bfloat16)


def near(shape, dtype=jnp.float32):
    return pltpu.VMEM(shape, dtype)


def mix_call(kernel, blocks, out_shape, operands, name):
    _, rows, width = blocks[0].shape
    count = sum(block.shape[0] for block in blocks)
    return pl.pallas_call(
        functools.partial(kernel, width // HEADS),
        out_shape=out_shape,
        in_specs=[VMEM] * (len(blocks) + len(operands)),
        out_specs=jax.tree.map(lambda _: VMEM, out_shape),
        scratch_shapes=[near((count * ceil_to(rows, 8), width))],
        compiler_params=pltpu.CompilerParams(vmem_limit_bytes=32 << 20),
        cost_estimate=pl.CostEstimate(
            flops=4 * count * rows * width * width, bytes_accessed=4 << 20, transcendentals=0
        ),
        name=name,
    )(*blocks, *operands)


def part_shapes(block):
    count, rows, width = block.shape
    total = count * ceil_to(rows, 8)
    return [near((total, LANES)), near((total, width))]


def mix_own(block, weights):
    _, rows, width = block.shape
    shapes = [near((ceil_to(rows, 8), width)), *part_shapes(block)]
    query, *part = mix_call(own_kernel, [block], shapes, weights, "mix_own")
    return query, tuple(part)


def mix_part(block, query, w_key, w_value):
    return mix_call(part_kernel, [block], part_shapes(block), (query, w_key, w_value), "mix_part")


def mix_last(blocks, query, w_key, w_value, parts):
    scores, values = zip(*parts)
    return mix_call(
        lambda head_width, *refs: last_kernel(head_width, len(parts), len(blocks), *refs),
        blocks,
        jax.ShapeDtypeStruct((1,) + blocks[0].shape[1:], blocks[0].dtype),
        (query, w_key, w_value, *scores, *values),
        "mix_last",
    )


def rounds(total):
    for step in range(1, total):
        if total & (total - 1) == 0:
            there = [(index, index ^ step) for index in range(total)]
        else:
            there = [(index, (index + step) % total) for index in range(total)]
        yield there, [(target, source) for source, target in there]


def chip_rounds(total):
    for there, back in rounds(total // 2):
        yield tuple(
            [(2 * source + core, 2 * target + core) for source, target in pairs for core in range(2)]
            for pairs in (there, back)
        )


def per_device(query_tokens, key_tokens, value_tokens, w_query, w_key, w_value):
    frame_total = lax.axis_size("frame")
    block_total = lax.axis_size("qblk")
    swap = [(index, index ^ 1) for index in range(frame_total)]
    own_block, near_query = load(key_tokens, value_tokens, query_tokens)
    blocks = [(own_block,)] + [(lax.ppermute(own_block, "qblk", there),) for there, _ in rounds(block_total)]
    paths = list(chip_rounds(frame_total))
    ready_query = lax.optimization_barrier((near_query, blocks[1 % len(blocks)][0]))[0]
    queries = [near_query] + [
        lax.ppermute(ready_query if step == 0 else near_query, "frame", there)
        for step, (there, _) in enumerate(paths)
    ]
    w_query, w_key, w_value = fetch((w_query, w_key, w_value))
    *queries, w_query, w_key, w_value = lax.optimization_barrier((*queries, w_query, w_key, w_value))
    turned = [
        lax.optimization_barrier((block, *queries, *blocks[index + 1 :]))[0]
        for index, block in enumerate(blocks)
    ]
    turned[:2] = [lax.optimization_barrier((block, *queries))[0] for block in blocks[:2]]
    other_blocks = [
        tuple(lax.ppermute(array, "frame", swap) for array in block) for block in turned
    ]
    *own, query = attention(queries, blocks)
    pooled = attention([query], other_blocks, own)
    own_query, part = mix_own(pooled[0], (w_query, w_key, w_value))
    if not paths:
        return mix_last([pooled[0]], own_query, w_key, w_value, [])
    arrived = [
        lax.ppermute(block, "frame", back)
        for block, (_, back) in zip(pooled[1:], paths)
    ]
    parts = [part]
    for block in arrived[:1:-1]:
        parts.append(mix_part(block, own_query, w_key, w_value))
    return mix_last(arrived[:2], own_query, w_key, w_value, parts)


def solution(mesh):
    in_specs = (
        P("frame", "qblk", None),
        P("frame", "qblk", None),
        P("frame", "qblk", None),
        P(),
        P(),
        P(),
    )
    out_specs = P("frame", "qblk", None)
    return jax.shard_map(
        per_device, mesh=mesh, in_specs=in_specs, out_specs=out_specs, check_vma=False
    )
```

```python
import functools
import math

import jax
import jax.numpy as jnp
from jax import lax
from jax.experimental import pallas as pl
from jax.experimental.pallas import tpu as pltpu
from jax.sharding import PartitionSpec as P

HEADS = 12
LANES = 128
VMEM = pl.BlockSpec(memory_space=pltpu.VMEM)
FAR = pl.BlockSpec(memory_space=pltpu.HBM)
NT = (((1,), (1,)), ((), ()))
TN = (((0,), (0,)), ((), ()))


def far(array):
    return pltpu.with_memory_space_constraint(array, pltpu.HBM)


def ceil_to(value, unit):
    return -(-value // unit) * unit


def stack_rows(blocks, stage, pitch):
    rows = blocks[0].shape[0]
    for index, block in enumerate(blocks):
        stage[pl.ds(index * pitch, rows), :] = block.astype(jnp.float32)
        end = stage.shape[0] if index == len(blocks) - 1 else (index + 1) * pitch
        gap = end - index * pitch - rows
        if gap:
            stage[pl.ds(index * pitch + rows, gap), :] = jnp.zeros((gap, stage.shape[1]), jnp.float32)
    return stage[...].astype(jnp.bfloat16)


def attend(query, key, value, key_count, head_width, out):
    per_slab = LANES // head_width
    factor = math.log2(math.e) / math.sqrt(head_width)
    query_total, key_total = query.shape[0], key.shape[0]
    head = lax.broadcasted_iota(jnp.int32, (query_total, LANES), 1) // head_width
    for at in range(0, query.shape[1], LANES):
        cut = slice(at, at + LANES)
        side = jnp.concatenate(
            [jnp.where(head == index, query[:, cut], 0) for index in range(per_slab)], axis=0
        )
        scores = lax.dot_general(key[:, cut], side, NT, preferred_element_type=jnp.float32)
        if key_count < key_total:
            place = lax.broadcasted_iota(jnp.int32, (key_total, 1), 0)
            scores = scores + jnp.where(place < key_count, 0.0, -1e30)
        top = jnp.max(scores, axis=0, keepdims=True)
        weights = jnp.exp2((scores - top) * factor)
        weights = weights * (1.0 / jnp.sum(weights, axis=0, keepdims=True))
        pooled = lax.dot_general(
            weights.astype(jnp.bfloat16), value[:, cut], TN, preferred_element_type=jnp.float32
        )
        mine = pooled[:query_total]
        for index in range(1, per_slab):
            mine = jnp.where(head == index, pooled[index * query_total : (index + 1) * query_total], mine)
        out[:, cut] = mine


def load_kernel(key, value, query, pair, near_query, sems):
    targets = (pair.at[0], pair.at[1], near_query.at[0])
    copies = [
        pltpu.make_async_copy(source.at[0], target, sems.at[index])
        for index, (source, target) in enumerate(zip((key, value, query), targets))
    ]
    for copy in copies:
        copy.start()
    for copy in copies:
        copy.wait()


def load(key, value, query):
    return pl.pallas_call(
        load_kernel,
        out_shape=[
            pltpu.VMEM((2,) + key.shape[1:], key.dtype),
            pltpu.VMEM(query.shape, query.dtype),
        ],
        in_specs=[FAR] * 3,
        out_specs=[VMEM] * 2,
        scratch_shapes=[pltpu.SemaphoreType.DMA((3,))],
        name="load",
    )(far(key), far(value), far(query))


def fetch_kernel(*refs):
    count = len(refs) // 2
    far_refs, held, sems = refs[:count], refs[count : 2 * count], refs[-1]
    copies = [
        pltpu.make_async_copy(source, target, sems.at[index])
        for index, (source, target) in enumerate(zip(far_refs, held))
    ]
    for copy in copies:
        copy.start()
    for copy in copies:
        copy.wait()


def fetch(weights):
    return pl.pallas_call(
        fetch_kernel,
        out_shape=[pltpu.VMEM(matrix.shape, matrix.dtype) for matrix in weights],
        in_specs=[FAR] * len(weights),
        out_specs=[VMEM] * len(weights),
        scratch_shapes=[pltpu.SemaphoreType.DMA((len(weights),))],
        compiler_params=pltpu.CompilerParams(vmem_limit_bytes=32 << 20),
        cost_estimate=pl.CostEstimate(flops=0, bytes_accessed=len(weights) << 21, transcendentals=0),
        name="fetch",
    )(*map(far, weights))


def attention_kernel(head_width, query_count, earlier_count, forms, *refs):
    queries, refs = refs[:query_count], refs[query_count:]
    keys, values = [], []
    for form in forms:
        keys.append(refs[0].at[0])
        values.append(refs[form - 1].at[2 - form])
        refs = refs[form:]
    *refs, key_stage, value_stage, query_stage = refs
    rows = keys[0].shape[-2]
    if earlier_count:
        earlier, outs = refs[:earlier_count], refs[earlier_count:]
        query = queries[0][...]
    else:
        earlier, (*outs, stacked) = (), refs
        query = stack_rows([ref[0] for ref in queries], query_stage, rows)
        stacked[...] = query
    key = stack_rows([ref[...] for ref in keys], key_stage, rows)
    value = stack_rows([ref[...] for ref in values], value_stage, rows)
    attend(query, key, value, len(keys) * rows, head_width, query_stage)
    for index, out in enumerate(outs):
        out[out.shape[0] - 1] = query_stage[pl.ds(index * rows, rows), :].astype(out.dtype)
    for out, ref in zip(outs, earlier):
        out[0] = ref[0]


def attention(queries, blocks, earlier=()):
    _, rows, width = blocks[0][0].shape
    count = len(earlier) or len(queries)
    query_total, key_total = ceil_to(count * rows, 16), ceil_to(len(blocks) * rows, 16)
    flops = 4 * count * rows * len(blocks) * rows * width
    shape = jax.ShapeDtypeStruct((2 if earlier else 1, rows, width), jnp.bfloat16)
    first = not earlier
    kernel = functools.partial(
        attention_kernel, width // HEADS, len(queries), len(earlier), [len(block) for block in blocks]
    )
    return pl.pallas_call(
        kernel,
        out_shape=[shape] * count + [near((query_total, width), jnp.bfloat16)] * first,
        in_specs=[VMEM] * (len(queries) + sum(map(len, blocks)) + len(earlier)),
        out_specs=[VMEM] * (count + first),
        scratch_shapes=[near((key_total, width))] * 2 + [near((query_total, width))],
        compiler_params=pltpu.CompilerParams(vmem_limit_bytes=48 << 20),
        cost_estimate=pl.CostEstimate(flops=flops, bytes_accessed=1 << 20, transcendentals=0),
        name="attention",
    )(*queries, *(array for block in blocks for array in block), *earlier)


def head_members(width, head_width):
    channel = lax.broadcasted_iota(jnp.int32, (width, LANES), 0) // head_width
    return (channel == lax.broadcasted_iota(jnp.int32, (width, LANES), 1)).astype(jnp.bfloat16)


def head_spread(width, head_width):
    channel = lax.broadcasted_iota(jnp.int32, (LANES, width), 1) // head_width
    return (channel == lax.broadcasted_iota(jnp.int32, (LANES, width), 0)).astype(jnp.bfloat16)


def project(rows, matrix):
    wide = jnp.dot(rows, matrix[...], preferred_element_type=jnp.float32)
    return wide.astype(jnp.bfloat16).astype(jnp.float32)


def score(query, pooled, w_key, head_width):
    path_key = project(pooled, w_key)
    pitch, width = query.shape
    product = jnp.concatenate(
        [path_key[at : at + pitch] * query for at in range(0, path_key.shape[0], pitch)], axis=0
    )
    member = head_members(width, head_width)
    high = product.astype(jnp.bfloat16)
    low = (product - high.astype(jnp.float32)).astype(jnp.bfloat16)
    scores = jnp.dot(high, member, preferred_element_type=jnp.float32) + jnp.dot(
        low, member, preferred_element_type=jnp.float32
    )
    return scores * (1.0 / math.sqrt(head_width))


def stack_pooled(ref, stage):
    return stack_rows([ref[index] for index in range(ref.shape[0])], stage, ceil_to(ref.shape[1], 8))


def own_kernel(head_width, block, w_query, w_key, w_value, query, scores, values, stage):
    pooled = stack_pooled(block, stage)
    rows, pitch = block.shape[1], query.shape[0]
    query[...] = project(pooled[: ceil_to(rows, 16)], w_query)[:pitch]
    scores[...] = score(query[...], pooled, w_key, head_width)
    values[...] = project(pooled, w_value)


def part_kernel(head_width, block, query, w_key, w_value, scores, values, stage):
    pooled = stack_pooled(block, stage)
    scores[...] = score(query[...], pooled, w_key, head_width)
    values[...] = project(pooled, w_value)


def last_kernel(head_width, earlier, count, *refs):
    blocks, (query, w_key, w_value), refs = refs[:count], refs[count : count + 3], refs[count + 3 :]
    score_refs, value_refs, (out, stage) = refs[:earlier], refs[earlier : 2 * earlier], refs[-2:]
    pitch, width = query.shape
    pooled = stack_rows([ref[index] for ref in blocks for index in range(ref.shape[0])], stage, pitch)
    score_parts = [ref[...] for ref in score_refs] + [score(query[...], pooled, w_key, head_width)]
    value_parts = [ref[...] for ref in value_refs] + [project(pooled, w_value)]
    places = [
        (part, at) for part in range(earlier + 1) for at in range(0, score_parts[part].shape[0], pitch)
    ]
    scores = [score_parts[part][at : at + pitch] for part, at in places]
    top = functools.reduce(jnp.maximum, scores)
    scores = [jnp.exp(part - top) for part in scores]
    share = 1.0 / functools.reduce(jnp.add, scores)
    weights = jnp.concatenate([part * share for part in scores], axis=0).astype(jnp.bfloat16)
    weights = jnp.dot(weights, head_spread(width, head_width), preferred_element_type=jnp.float32)
    mixed = functools.reduce(
        jnp.add,
        [
            weights[index * pitch : (index + 1) * pitch] * value_parts[part][at : at + pitch]
            for index, (part, at) in enumerate(places)
        ],
    )
    out[0] = mixed[: blocks[0].shape[1]].astype(jnp.bfloat16)


def near(shape, dtype=jnp.float32):
    return pltpu.VMEM(shape, dtype)


def mix_call(kernel, blocks, out_shape, operands, name):
    _, rows, width = blocks[0].shape
    count = sum(block.shape[0] for block in blocks)
    return pl.pallas_call(
        functools.partial(kernel, width // HEADS),
        out_shape=out_shape,
        in_specs=[VMEM] * (len(blocks) + len(operands)),
        out_specs=jax.tree.map(lambda _: VMEM, out_shape),
        scratch_shapes=[near((count * ceil_to(rows, 8), width))],
        compiler_params=pltpu.CompilerParams(vmem_limit_bytes=32 << 20),
        cost_estimate=pl.CostEstimate(
            flops=4 * count * rows * width * width, bytes_accessed=4 << 20, transcendentals=0
        ),
        name=name,
    )(*blocks, *operands)


def part_shapes(block):
    count, rows, width = block.shape
    total = count * ceil_to(rows, 8)
    return [near((total, LANES)), near((total, width))]


def mix_own(block, weights):
    _, rows, width = block.shape
    shapes = [near((ceil_to(rows, 8), width)), *part_shapes(block)]
    query, *part = mix_call(own_kernel, [block], shapes, weights, "mix_own")
    return query, tuple(part)


def mix_part(block, query, w_key, w_value):
    return mix_call(part_kernel, [block], part_shapes(block), (query, w_key, w_value), "mix_part")


def mix_last(blocks, query, w_key, w_value, parts):
    scores, values = zip(*parts)
    return mix_call(
        lambda head_width, *refs: last_kernel(head_width, len(parts), len(blocks), *refs),
        blocks,
        jax.ShapeDtypeStruct((1,) + blocks[0].shape[1:], blocks[0].dtype),
        (query, w_key, w_value, *scores, *values),
        "mix_last",
    )


def rounds(total):
    for step in range(1, total):
        if total & (total - 1) == 0:
            there = [(index, index ^ step) for index in range(total)]
        else:
            there = [(index, (index + step) % total) for index in range(total)]
        yield there, [(target, source) for source, target in there]


def chip_rounds(total):
    for there, back in rounds(total // 2):
        yield tuple(
            [(2 * source + core, 2 * target + core) for source, target in pairs for core in range(2)]
            for pairs in (there, back)
        )


def per_device(query_tokens, key_tokens, value_tokens, w_query, w_key, w_value):
    frame_total = lax.axis_size("frame")
    block_total = lax.axis_size("qblk")
    swap = [(index, index ^ 1) for index in range(frame_total)]
    own_block, near_query = load(key_tokens, value_tokens, query_tokens)
    steps = [there for there, _ in rounds(block_total)]
    order = steps[1:] + steps[:1]
    blocks = [(own_block,)] + [(lax.ppermute(own_block, "qblk", there),) for there in order]
    paths = list(chip_rounds(frame_total))
    queries = [near_query] + [lax.ppermute(near_query, "frame", there) for there, _ in paths]
    w_query, w_key, w_value = fetch((w_query, w_key, w_value))
    *queries, w_query, w_key, w_value = lax.optimization_barrier((*queries, w_query, w_key, w_value))
    turned = [
        lax.optimization_barrier((block, *queries, *blocks[index + 1 :]))[0]
        for index, block in enumerate(blocks)
    ]
    turned[:2] = [lax.optimization_barrier((block, *queries))[0] for block in blocks[:2]]
    other_blocks = [
        tuple(lax.ppermute(array, "frame", swap) for array in block) for block in turned
    ]
    *own, query = attention(queries, blocks)
    pooled = attention([query], other_blocks, own)
    own_query, part = mix_own(pooled[0], (w_query, w_key, w_value))
    if not paths:
        return mix_last([pooled[0]], own_query, w_key, w_value, [])
    arrived = [
        lax.ppermute(block, "frame", back)
        for block, (_, back) in zip(pooled[1:], paths)
    ]
    parts = [part]
    for block in arrived[:1:-1]:
        parts.append(mix_part(block, own_query, w_key, w_value))
    return mix_last(arrived[:2], own_query, w_key, w_value, parts)


def solution(mesh):
    in_specs = (
        P("frame", "qblk", None),
        P("frame", "qblk", None),
        P("frame", "qblk", None),
        P(),
        P(),
        P(),
    )
    out_specs = P("frame", "qblk", None)
    return jax.shard_map(
        per_device, mesh=mesh, in_specs=in_specs, out_specs=out_specs, check_vma=False
    )
```

```python
import functools
import math

import jax
import jax.numpy as jnp
from jax import lax
from jax.experimental import pallas as pl
from jax.experimental.pallas import tpu as pltpu
from jax.sharding import PartitionSpec as P

HEADS = 12
LANES = 128
VMEM = pl.BlockSpec(memory_space=pltpu.VMEM)
FAR = pl.BlockSpec(memory_space=pltpu.HBM)
NT = (((1,), (1,)), ((), ()))
TN = (((0,), (0,)), ((), ()))


def far(array):
    return pltpu.with_memory_space_constraint(array, pltpu.HBM)


def ceil_to(value, unit):
    return -(-value // unit) * unit


def stack_rows(blocks, stage, pitch):
    rows = blocks[0].shape[0]
    for index, block in enumerate(blocks):
        stage[pl.ds(index * pitch, rows), :] = block.astype(jnp.float32)
        end = stage.shape[0] if index == len(blocks) - 1 else (index + 1) * pitch
        gap = end - index * pitch - rows
        if gap:
            stage[pl.ds(index * pitch + rows, gap), :] = jnp.zeros((gap, stage.shape[1]), jnp.float32)
    return stage[...].astype(jnp.bfloat16)


def halves(pair, apart):
    rows = pair.shape[0] // 2
    apart[...] = pair[...].astype(jnp.float32)
    return [apart[pl.ds(at, rows), :] for at in (0, rows)]


def attend(query, key, value, key_count, head_width, out):
    per_slab = LANES // head_width
    factor = math.log2(math.e) / math.sqrt(head_width)
    query_total, key_total = query.shape[0], key.shape[0]
    head = lax.broadcasted_iota(jnp.int32, (query_total, LANES), 1) // head_width
    for at in range(0, query.shape[1], LANES):
        cut = slice(at, at + LANES)
        side = jnp.concatenate(
            [jnp.where(head == index, query[:, cut], 0) for index in range(per_slab)], axis=0
        )
        scores = lax.dot_general(key[:, cut], side, NT, preferred_element_type=jnp.float32)
        if key_count < key_total:
            place = lax.broadcasted_iota(jnp.int32, (key_total, 1), 0)
            scores = scores + jnp.where(place < key_count, 0.0, -1e30)
        top = jnp.max(scores, axis=0, keepdims=True)
        weights = jnp.exp2((scores - top) * factor)
        weights = weights * (1.0 / jnp.sum(weights, axis=0, keepdims=True))
        pooled = lax.dot_general(
            weights.astype(jnp.bfloat16), value[:, cut], TN, preferred_element_type=jnp.float32
        )
        mine = pooled[:query_total]
        for index in range(1, per_slab):
            mine = jnp.where(head == index, pooled[index * query_total : (index + 1) * query_total], mine)
        out[:, cut] = mine


def load_kernel(key, value, query, pair, near_query, near_key, near_value, apart, sems):
    targets = (near_key, near_value, near_query.at[0])
    copies = [
        pltpu.make_async_copy(source.at[0], target, sems.at[index])
        for index, (source, target) in enumerate(zip((key, value, query), targets))
    ]
    for copy in copies:
        copy.start()
    for copy in copies:
        copy.wait()
    pair[...] = stack_rows([near_key[...], near_value[...]], apart, near_key.shape[0])


def load(key, value, query):
    _, rows, width = key.shape
    return pl.pallas_call(
        load_kernel,
        out_shape=[near((2 * rows, width), key.dtype), near(query.shape, query.dtype)],
        in_specs=[FAR] * 3,
        out_specs=[VMEM] * 2,
        scratch_shapes=[
            near((rows, width), key.dtype),
            near((rows, width), key.dtype),
            near((2 * rows, width)),
            pltpu.SemaphoreType.DMA((3,)),
        ],
        name="load",
    )(far(key), far(value), far(query))


def fetch_kernel(*refs):
    count = len(refs) // 2
    far_refs, held, sems = refs[:count], refs[count : 2 * count], refs[-1]
    copies = [
        pltpu.make_async_copy(source, target, sems.at[index])
        for index, (source, target) in enumerate(zip(far_refs, held))
    ]
    for copy in copies:
        copy.start()
    for copy in copies:
        copy.wait()


def fetch(weights):
    return pl.pallas_call(
        fetch_kernel,
        out_shape=[pltpu.VMEM(matrix.shape, matrix.dtype) for matrix in weights],
        in_specs=[FAR] * len(weights),
        out_specs=[VMEM] * len(weights),
        scratch_shapes=[pltpu.SemaphoreType.DMA((len(weights),))],
        compiler_params=pltpu.CompilerParams(vmem_limit_bytes=32 << 20),
        cost_estimate=pl.CostEstimate(flops=0, bytes_accessed=len(weights) << 21, transcendentals=0),
        name="fetch",
    )(*map(far, weights))


def attention_kernel(head_width, query_count, earlier_count, block_count, *refs):
    queries, refs = refs[:query_count], refs[query_count:]
    blocks, refs = refs[:block_count], refs[block_count:]
    *refs, key_stage, value_stage, query_stage, apart = refs
    rows = blocks[0].shape[0] // 2
    if earlier_count:
        earlier, outs = refs[:earlier_count], refs[earlier_count:]
        query = queries[0][...]
    else:
        earlier, (*outs, stacked) = (), refs
        query = stack_rows([ref[0] for ref in queries], query_stage, rows)
        stacked[...] = query
    keys, values = zip(*[halves(ref, apart) for ref in blocks])
    key = stack_rows(keys, key_stage, rows)
    value = stack_rows(values, value_stage, rows)
    attend(query, key, value, block_count * rows, head_width, query_stage)
    for index, out in enumerate(outs):
        mine = query_stage[pl.ds(index * rows, rows), :]
        if earlier:
            out[...] = stack_rows([earlier[index][0], mine], apart, rows)
        else:
            out[0] = mine.astype(out.dtype)


def attention(queries, blocks, earlier=()):
    width = blocks[0].shape[1]
    rows = blocks[0].shape[0] // 2
    count = len(earlier) or len(queries)
    query_total, key_total = ceil_to(count * rows, 16), ceil_to(len(blocks) * rows, 16)
    flops = 4 * count * rows * len(blocks) * rows * width
    shape = jax.ShapeDtypeStruct((2 * rows, width) if earlier else (1, rows, width), jnp.bfloat16)
    first = not earlier
    kernel = functools.partial(
        attention_kernel, width // HEADS, len(queries), len(earlier), len(blocks)
    )
    return pl.pallas_call(
        kernel,
        out_shape=[shape] * count + [near((query_total, width), jnp.bfloat16)] * first,
        in_specs=[VMEM] * (len(queries) + len(blocks) + len(earlier)),
        out_specs=[VMEM] * (count + first),
        scratch_shapes=[near((key_total, width))] * 2
        + [near((query_total, width)), near((2 * rows, width))],
        compiler_params=pltpu.CompilerParams(vmem_limit_bytes=48 << 20),
        cost_estimate=pl.CostEstimate(flops=flops, bytes_accessed=1 << 20, transcendentals=0),
        name="attention",
    )(*queries, *blocks, *earlier)


def head_members(width, head_width):
    channel = lax.broadcasted_iota(jnp.int32, (width, LANES), 0) // head_width
    return (channel == lax.broadcasted_iota(jnp.int32, (width, LANES), 1)).astype(jnp.bfloat16)


def head_spread(width, head_width):
    channel = lax.broadcasted_iota(jnp.int32, (LANES, width), 1) // head_width
    return (channel == lax.broadcasted_iota(jnp.int32, (LANES, width), 0)).astype(jnp.bfloat16)


def project(rows, matrix):
    wide = jnp.dot(rows, matrix[...], preferred_element_type=jnp.float32)
    return wide.astype(jnp.bfloat16).astype(jnp.float32)


def score(query, pooled, w_key, head_width):
    path_key = project(pooled, w_key)
    pitch, width = query.shape
    product = jnp.concatenate(
        [path_key[at : at + pitch] * query for at in range(0, path_key.shape[0], pitch)], axis=0
    )
    member = head_members(width, head_width)
    high = product.astype(jnp.bfloat16)
    low = (product - high.astype(jnp.float32)).astype(jnp.bfloat16)
    scores = jnp.dot(high, member, preferred_element_type=jnp.float32) + jnp.dot(
        low, member, preferred_element_type=jnp.float32
    )
    return scores * (1.0 / math.sqrt(head_width))


def stack_pooled(refs, stage, apart, pitch):
    return stack_rows([half for ref in refs for half in halves(ref, apart)], stage, pitch)


def own_kernel(head_width, block, w_query, w_key, w_value, query, scores, values, stage, apart):
    rows, pitch = block.shape[0] // 2, query.shape[0]
    pooled = stack_pooled([block], stage, apart, pitch)
    query[...] = project(pooled[: ceil_to(rows, 16)], w_query)[:pitch]
    scores[...] = score(query[...], pooled, w_key, head_width)
    values[...] = project(pooled, w_value)


def part_kernel(head_width, block, query, w_key, w_value, scores, values, stage, apart):
    pooled = stack_pooled([block], stage, apart, query.shape[0])
    scores[...] = score(query[...], pooled, w_key, head_width)
    values[...] = project(pooled, w_value)


def last_kernel(head_width, earlier, count, *refs):
    blocks, (query, w_key, w_value), refs = refs[:count], refs[count : count + 3], refs[count + 3 :]
    score_refs, value_refs = refs[:earlier], refs[earlier : 2 * earlier]
    out, stage, apart = refs[-3:]
    pitch, width = query.shape
    pooled = stack_pooled(blocks, stage, apart, pitch)
    score_parts = [ref[...] for ref in score_refs] + [score(query[...], pooled, w_key, head_width)]
    value_parts = [ref[...] for ref in value_refs] + [project(pooled, w_value)]
    places = [
        (part, at) for part in range(earlier + 1) for at in range(0, score_parts[part].shape[0], pitch)
    ]
    scores = [score_parts[part][at : at + pitch] for part, at in places]
    top = functools.reduce(jnp.maximum, scores)
    scores = [jnp.exp(part - top) for part in scores]
    share = 1.0 / functools.reduce(jnp.add, scores)
    weights = jnp.concatenate([part * share for part in scores], axis=0).astype(jnp.bfloat16)
    weights = jnp.dot(weights, head_spread(width, head_width), preferred_element_type=jnp.float32)
    mixed = functools.reduce(
        jnp.add,
        [
            weights[index * pitch : (index + 1) * pitch] * value_parts[part][at : at + pitch]
            for index, (part, at) in enumerate(places)
        ],
    )
    out[0] = mixed[: blocks[0].shape[0] // 2].astype(jnp.bfloat16)


def near(shape, dtype=jnp.float32):
    return pltpu.VMEM(shape, dtype)


def mix_call(kernel, blocks, out_shape, operands, name):
    width = blocks[0].shape[1]
    rows = blocks[0].shape[0] // 2
    count = 2 * len(blocks)
    return pl.pallas_call(
        functools.partial(kernel, width // HEADS),
        out_shape=out_shape,
        in_specs=[VMEM] * (len(blocks) + len(operands)),
        out_specs=jax.tree.map(lambda _: VMEM, out_shape),
        scratch_shapes=[near((count * ceil_to(rows, 8), width)), near((2 * rows, width))],
        compiler_params=pltpu.CompilerParams(vmem_limit_bytes=32 << 20),
        cost_estimate=pl.CostEstimate(
            flops=4 * count * rows * width * width, bytes_accessed=4 << 20, transcendentals=0
        ),
        name=name,
    )(*blocks, *operands)


def part_shapes(block):
    width = block.shape[1]
    total = 2 * ceil_to(block.shape[0] // 2, 8)
    return [near((total, LANES)), near((total, width))]


def mix_own(block, weights):
    shapes = [near((ceil_to(block.shape[0] // 2, 8), block.shape[1])), *part_shapes(block)]
    query, *part = mix_call(own_kernel, [block], shapes, weights, "mix_own")
    return query, tuple(part)


def mix_part(block, query, w_key, w_value):
    return mix_call(part_kernel, [block], part_shapes(block), (query, w_key, w_value), "mix_part")


def mix_last(blocks, query, w_key, w_value, parts):
    scores, values = zip(*parts)
    return mix_call(
        lambda head_width, *refs: last_kernel(head_width, len(parts), len(blocks), *refs),
        blocks,
        jax.ShapeDtypeStruct((1, blocks[0].shape[0] // 2, blocks[0].shape[1]), blocks[0].dtype),
        (query, w_key, w_value, *scores, *values),
        "mix_last",
    )


def rounds(total):
    for step in range(1, total):
        if total & (total - 1) == 0:
            there = [(index, index ^ step) for index in range(total)]
        else:
            there = [(index, (index + step) % total) for index in range(total)]
        yield there, [(target, source) for source, target in there]


def chip_rounds(total):
    for there, back in rounds(total // 2):
        yield tuple(
            [(2 * source + core, 2 * target + core) for source, target in pairs for core in range(2)]
            for pairs in (there, back)
        )


def per_device(query_tokens, key_tokens, value_tokens, w_query, w_key, w_value):
    frame_total = lax.axis_size("frame")
    block_total = lax.axis_size("qblk")
    swap = [(index, index ^ 1) for index in range(frame_total)]
    own_block, near_query = load(key_tokens, value_tokens, query_tokens)
    steps = [there for there, _ in rounds(block_total)]
    order = steps[1:] + steps[:1]
    blocks = [own_block] + [lax.ppermute(own_block, "qblk", there) for there in order]
    paths = list(chip_rounds(frame_total))
    queries = [near_query] + [lax.ppermute(near_query, "frame", there) for there, _ in paths]
    w_query, w_key, w_value = fetch((w_query, w_key, w_value))
    *queries, w_query, w_key, w_value = lax.optimization_barrier((*queries, w_query, w_key, w_value))
    turned = [
        lax.optimization_barrier((block, *queries, *blocks[index + 1 :]))[0]
        for index, block in enumerate(blocks)
    ]
    turned[:2] = [lax.optimization_barrier((block, *queries))[0] for block in blocks[:2]]
    other_blocks = [lax.ppermute(block, "frame", swap) for block in turned]
    *own, query = attention(queries, blocks)
    pooled = attention([query], other_blocks, own)
    own_query, part = mix_own(pooled[0], (w_query, w_key, w_value))
    if not paths:
        return mix_last([pooled[0]], own_query, w_key, w_value, [])
    arrived = [
        lax.ppermute(block, "frame", back)
        for block, (_, back) in zip(pooled[1:], paths)
    ]
    parts = [part]
    for block in arrived[:1:-1]:
        parts.append(mix_part(block, own_query, w_key, w_value))
    return mix_last(arrived[:2], own_query, w_key, w_value, parts)


def solution(mesh):
    in_specs = (
        P("frame", "qblk", None),
        P("frame", "qblk", None),
        P("frame", "qblk", None),
        P(),
        P(),
        P(),
    )
    out_specs = P("frame", "qblk", None)
    return jax.shard_map(
        per_device, mesh=mesh, in_specs=in_specs, out_specs=out_specs, check_vma=False
    )
```

```python
import functools
import math

import jax
import jax.numpy as jnp
from jax import lax
from jax.experimental import pallas as pl
from jax.experimental.pallas import tpu as pltpu
from jax.sharding import PartitionSpec as P

HEADS = 12
LANES = 128
VMEM = pl.BlockSpec(memory_space=pltpu.VMEM)
FAR = pl.BlockSpec(memory_space=pltpu.HBM)
NT = (((1,), (1,)), ((), ()))
TN = (((0,), (0,)), ((), ()))


def far(array):
    return pltpu.with_memory_space_constraint(array, pltpu.HBM)


def ceil_to(value, unit):
    return -(-value // unit) * unit


def stack_rows(blocks, stage, pitch):
    rows = blocks[0].shape[0]
    for index, block in enumerate(blocks):
        stage[pl.ds(index * pitch, rows), :] = block.astype(jnp.float32)
        end = stage.shape[0] if index == len(blocks) - 1 else (index + 1) * pitch
        gap = end - index * pitch - rows
        if gap:
            stage[pl.ds(index * pitch + rows, gap), :] = jnp.zeros((gap, stage.shape[1]), jnp.float32)
    return stage[...].astype(jnp.bfloat16)


def halves(pair, apart):
    rows = pair.shape[0] // 2
    apart[...] = pair[...].astype(jnp.float32)
    return [apart[pl.ds(at, rows), :] for at in (0, rows)]


def attend(query, key, value, key_count, head_width, out):
    per_slab = LANES // head_width
    factor = math.log2(math.e) / math.sqrt(head_width)
    query_total, key_total = query.shape[0], key.shape[0]
    head = lax.broadcasted_iota(jnp.int32, (query_total, LANES), 1) // head_width
    for at in range(0, query.shape[1], LANES):
        cut = slice(at, at + LANES)
        side = jnp.concatenate(
            [jnp.where(head == index, query[:, cut], 0) for index in range(per_slab)], axis=0
        )
        scores = lax.dot_general(key[:, cut], side, NT, preferred_element_type=jnp.float32)
        if key_count < key_total:
            place = lax.broadcasted_iota(jnp.int32, (key_total, 1), 0)
            scores = scores + jnp.where(place < key_count, 0.0, -1e30)
        top = jnp.max(scores, axis=0, keepdims=True)
        weights = jnp.exp2((scores - top) * factor)
        weights = weights * (1.0 / jnp.sum(weights, axis=0, keepdims=True))
        pooled = lax.dot_general(
            weights.astype(jnp.bfloat16), value[:, cut], TN, preferred_element_type=jnp.float32
        )
        mine = pooled[:query_total]
        for index in range(1, per_slab):
            mine = jnp.where(head == index, pooled[index * query_total : (index + 1) * query_total], mine)
        out[:, cut] = mine


def load_kernel(key, value, query, pair, packed, near_key, near_value, near_query, apart, apart_query, sems):
    targets = (near_key, near_value, near_query)
    copies = [
        pltpu.make_async_copy(source.at[0], target, sems.at[index])
        for index, (source, target) in enumerate(zip((key, value, query), targets))
    ]
    for copy in copies:
        copy.start()
    for copy in copies:
        copy.wait()
    pair[...] = stack_rows([near_key[...], near_value[...]], apart, near_key.shape[0])
    middle = near_query.shape[1] // 2
    sides = [near_query[:, :middle], near_query[:, middle:]]
    packed[...] = stack_rows(sides, apart_query, near_query.shape[0])


def load(key, value, query):
    _, rows, width = key.shape
    return pl.pallas_call(
        load_kernel,
        out_shape=[near((2 * rows, width), key.dtype), near((2 * rows, width // 2), query.dtype)],
        in_specs=[FAR] * 3,
        out_specs=[VMEM] * 2,
        scratch_shapes=[
            near((rows, width), key.dtype),
            near((rows, width), key.dtype),
            near((rows, width), query.dtype),
            near((2 * rows, width)),
            near((2 * rows, width // 2)),
            pltpu.SemaphoreType.DMA((3,)),
        ],
        name="load",
    )(far(key), far(value), far(query))


def fetch_kernel(*refs):
    count = len(refs) // 2
    far_refs, held, sems = refs[:count], refs[count : 2 * count], refs[-1]
    copies = [
        pltpu.make_async_copy(source, target, sems.at[index])
        for index, (source, target) in enumerate(zip(far_refs, held))
    ]
    for copy in copies:
        copy.start()
    for copy in copies:
        copy.wait()


def fetch(weights):
    return pl.pallas_call(
        fetch_kernel,
        out_shape=[pltpu.VMEM(matrix.shape, matrix.dtype) for matrix in weights],
        in_specs=[FAR] * len(weights),
        out_specs=[VMEM] * len(weights),
        scratch_shapes=[pltpu.SemaphoreType.DMA((len(weights),))],
        compiler_params=pltpu.CompilerParams(vmem_limit_bytes=32 << 20),
        cost_estimate=pl.CostEstimate(flops=0, bytes_accessed=len(weights) << 21, transcendentals=0),
        name="fetch",
    )(*map(far, weights))


def attention_kernel(head_width, query_count, earlier_count, block_count, *refs):
    queries, refs = refs[:query_count], refs[query_count:]
    blocks, refs = refs[:block_count], refs[block_count:]
    *refs, key_stage, value_stage, query_stage, apart, apart_query = refs
    rows = blocks[0].shape[0] // 2
    if earlier_count:
        earlier, outs = refs[:earlier_count], refs[earlier_count:]
        query = queries[0][...]
    else:
        earlier, (*outs, stacked) = (), refs
        sides = [halves(ref, apart_query) for ref in queries]
        query = stack_rows([jnp.concatenate(side, axis=1) for side in sides], query_stage, rows)
        stacked[...] = query
    keys, values = zip(*[halves(ref, apart) for ref in blocks])
    key = stack_rows(keys, key_stage, rows)
    value = stack_rows(values, value_stage, rows)
    attend(query, key, value, block_count * rows, head_width, query_stage)
    for index, out in enumerate(outs):
        mine = query_stage[pl.ds(index * rows, rows), :]
        if earlier:
            out[...] = stack_rows([earlier[index][0], mine], apart, rows)
        else:
            out[0] = mine.astype(out.dtype)


def attention(queries, blocks, earlier=()):
    width = blocks[0].shape[1]
    rows = blocks[0].shape[0] // 2
    count = len(earlier) or len(queries)
    query_total, key_total = ceil_to(count * rows, 16), ceil_to(len(blocks) * rows, 16)
    flops = 4 * count * rows * len(blocks) * rows * width
    shape = jax.ShapeDtypeStruct((2 * rows, width) if earlier else (1, rows, width), jnp.bfloat16)
    first = not earlier
    kernel = functools.partial(
        attention_kernel, width // HEADS, len(queries), len(earlier), len(blocks)
    )
    return pl.pallas_call(
        kernel,
        out_shape=[shape] * count + [near((query_total, width), jnp.bfloat16)] * first,
        in_specs=[VMEM] * (len(queries) + len(blocks) + len(earlier)),
        out_specs=[VMEM] * (count + first),
        scratch_shapes=[near((key_total, width))] * 2
        + [near((query_total, width)), near((2 * rows, width)), near((2 * rows, width // 2))],
        compiler_params=pltpu.CompilerParams(vmem_limit_bytes=48 << 20),
        cost_estimate=pl.CostEstimate(flops=flops, bytes_accessed=1 << 20, transcendentals=0),
        name="attention",
    )(*queries, *blocks, *earlier)


def head_members(width, head_width):
    channel = lax.broadcasted_iota(jnp.int32, (width, LANES), 0) // head_width
    return (channel == lax.broadcasted_iota(jnp.int32, (width, LANES), 1)).astype(jnp.bfloat16)


def head_spread(width, head_width):
    channel = lax.broadcasted_iota(jnp.int32, (LANES, width), 1) // head_width
    return (channel == lax.broadcasted_iota(jnp.int32, (LANES, width), 0)).astype(jnp.bfloat16)


def project(rows, matrix):
    wide = jnp.dot(rows, matrix[...], preferred_element_type=jnp.float32)
    return wide.astype(jnp.bfloat16).astype(jnp.float32)


def score(query, pooled, w_key, head_width):
    path_key = project(pooled, w_key)
    pitch, width = query.shape
    product = jnp.concatenate(
        [path_key[at : at + pitch] * query for at in range(0, path_key.shape[0], pitch)], axis=0
    )
    member = head_members(width, head_width)
    high = product.astype(jnp.bfloat16)
    low = (product - high.astype(jnp.float32)).astype(jnp.bfloat16)
    scores = jnp.dot(high, member, preferred_element_type=jnp.float32) + jnp.dot(
        low, member, preferred_element_type=jnp.float32
    )
    return scores * (1.0 / math.sqrt(head_width))


def stack_pooled(refs, stage, apart, pitch):
    return stack_rows([half for ref in refs for half in halves(ref, apart)], stage, pitch)


def own_kernel(head_width, block, w_query, w_key, w_value, query, scores, values, stage, apart):
    rows, pitch = block.shape[0] // 2, query.shape[0]
    pooled = stack_pooled([block], stage, apart, pitch)
    query[...] = project(pooled[: ceil_to(rows, 16)], w_query)[:pitch]
    scores[...] = score(query[...], pooled, w_key, head_width)
    values[...] = project(pooled, w_value)


def part_kernel(head_width, block, query, w_key, w_value, scores, values, stage, apart):
    pooled = stack_pooled([block], stage, apart, query.shape[0])
    scores[...] = score(query[...], pooled, w_key, head_width)
    values[...] = project(pooled, w_value)


def last_kernel(head_width, earlier, count, *refs):
    blocks, (query, w_key, w_value), refs = refs[:count], refs[count : count + 3], refs[count + 3 :]
    score_refs, value_refs = refs[:earlier], refs[earlier : 2 * earlier]
    out, stage, apart = refs[-3:]
    pitch, width = query.shape
    pooled = stack_pooled(blocks, stage, apart, pitch)
    score_parts = [ref[...] for ref in score_refs] + [score(query[...], pooled, w_key, head_width)]
    value_parts = [ref[...] for ref in value_refs] + [project(pooled, w_value)]
    places = [
        (part, at) for part in range(earlier + 1) for at in range(0, score_parts[part].shape[0], pitch)
    ]
    scores = [score_parts[part][at : at + pitch] for part, at in places]
    top = functools.reduce(jnp.maximum, scores)
    scores = [jnp.exp(part - top) for part in scores]
    share = 1.0 / functools.reduce(jnp.add, scores)
    weights = jnp.concatenate([part * share for part in scores], axis=0).astype(jnp.bfloat16)
    weights = jnp.dot(weights, head_spread(width, head_width), preferred_element_type=jnp.float32)
    mixed = functools.reduce(
        jnp.add,
        [
            weights[index * pitch : (index + 1) * pitch] * value_parts[part][at : at + pitch]
            for index, (part, at) in enumerate(places)
        ],
    )
    out[0] = mixed[: blocks[0].shape[0] // 2].astype(jnp.bfloat16)


def near(shape, dtype=jnp.float32):
    return pltpu.VMEM(shape, dtype)


def mix_call(kernel, blocks, out_shape, operands, name):
    width = blocks[0].shape[1]
    rows = blocks[0].shape[0] // 2
    count = 2 * len(blocks)
    return pl.pallas_call(
        functools.partial(kernel, width // HEADS),
        out_shape=out_shape,
        in_specs=[VMEM] * (len(blocks) + len(operands)),
        out_specs=jax.tree.map(lambda _: VMEM, out_shape),
        scratch_shapes=[near((count * ceil_to(rows, 8), width)), near((2 * rows, width))],
        compiler_params=pltpu.CompilerParams(vmem_limit_bytes=32 << 20),
        cost_estimate=pl.CostEstimate(
            flops=4 * count * rows * width * width, bytes_accessed=4 << 20, transcendentals=0
        ),
        name=name,
    )(*blocks, *operands)


def part_shapes(block):
    width = block.shape[1]
    total = 2 * ceil_to(block.shape[0] // 2, 8)
    return [near((total, LANES)), near((total, width))]


def mix_own(block, weights):
    shapes = [near((ceil_to(block.shape[0] // 2, 8), block.shape[1])), *part_shapes(block)]
    query, *part = mix_call(own_kernel, [block], shapes, weights, "mix_own")
    return query, tuple(part)


def mix_part(block, query, w_key, w_value):
    return mix_call(part_kernel, [block], part_shapes(block), (query, w_key, w_value), "mix_part")


def mix_last(blocks, query, w_key, w_value, parts):
    scores, values = zip(*parts)
    return mix_call(
        lambda head_width, *refs: last_kernel(head_width, len(parts), len(blocks), *refs),
        blocks,
        jax.ShapeDtypeStruct((1, blocks[0].shape[0] // 2, blocks[0].shape[1]), blocks[0].dtype),
        (query, w_key, w_value, *scores, *values),
        "mix_last",
    )


def rounds(total):
    for step in range(1, total):
        if total & (total - 1) == 0:
            there = [(index, index ^ step) for index in range(total)]
        else:
            there = [(index, (index + step) % total) for index in range(total)]
        yield there, [(target, source) for source, target in there]


def chip_rounds(total):
    for there, back in rounds(total // 2):
        yield tuple(
            [(2 * source + core, 2 * target + core) for source, target in pairs for core in range(2)]
            for pairs in (there, back)
        )


def per_device(query_tokens, key_tokens, value_tokens, w_query, w_key, w_value):
    frame_total = lax.axis_size("frame")
    block_total = lax.axis_size("qblk")
    swap = [(index, index ^ 1) for index in range(frame_total)]
    own_block, near_query = load(key_tokens, value_tokens, query_tokens)
    steps = [there for there, _ in rounds(block_total)]
    order = steps[1:] + steps[:1]
    blocks = [own_block] + [lax.ppermute(own_block, "qblk", there) for there in order]
    paths = list(chip_rounds(frame_total))
    queries = [near_query] + [lax.ppermute(near_query, "frame", there) for there, _ in paths]
    w_query, w_key, w_value = fetch((w_query, w_key, w_value))
    *queries, w_query, w_key, w_value = lax.optimization_barrier((*queries, w_query, w_key, w_value))
    turned = [
        lax.optimization_barrier((block, *queries, *blocks[index + 1 :]))[0]
        for index, block in enumerate(blocks)
    ]
    turned[:2] = [lax.optimization_barrier((block, *queries))[0] for block in blocks[:2]]
    other_blocks = [lax.ppermute(block, "frame", swap) for block in turned]
    *own, query = attention(queries, blocks)
    pooled = attention([query], other_blocks, own)
    own_query, part = mix_own(pooled[0], (w_query, w_key, w_value))
    if not paths:
        return mix_last([pooled[0]], own_query, w_key, w_value, [])
    arrived = [
        lax.ppermute(block, "frame", back)
        for block, (_, back) in zip(pooled[1:], paths)
    ]
    parts = [part]
    for block in arrived[:1:-1]:
        parts.append(mix_part(block, own_query, w_key, w_value))
    return mix_last(arrived[:2], own_query, w_key, w_value, parts)


def solution(mesh):
    in_specs = (
        P("frame", "qblk", None),
        P("frame", "qblk", None),
        P("frame", "qblk", None),
        P(),
        P(),
        P(),
    )
    out_specs = P("frame", "qblk", None)
    return jax.shard_map(
        per_device, mesh=mesh, in_specs=in_specs, out_specs=out_specs, check_vma=False
    )
```

```python
import functools
import math

import jax
import jax.numpy as jnp
from jax import lax
from jax.experimental import pallas as pl
from jax.experimental.pallas import tpu as pltpu
from jax.sharding import PartitionSpec as P

HEADS = 12
LANES = 128
VMEM = pl.BlockSpec(memory_space=pltpu.VMEM)
FAR = pl.BlockSpec(memory_space=pltpu.HBM)
NT = (((1,), (1,)), ((), ()))
TN = (((0,), (0,)), ((), ()))


def far(array):
    return pltpu.with_memory_space_constraint(array, pltpu.HBM)


def ceil_to(value, unit):
    return -(-value // unit) * unit


def stack_rows(blocks, stage, pitch):
    rows = blocks[0].shape[0]
    for index, block in enumerate(blocks):
        stage[pl.ds(index * pitch, rows), :] = block.astype(jnp.float32)
        end = stage.shape[0] if index == len(blocks) - 1 else (index + 1) * pitch
        gap = end - index * pitch - rows
        if gap:
            stage[pl.ds(index * pitch + rows, gap), :] = jnp.zeros((gap, stage.shape[1]), jnp.float32)
    return stage[...].astype(jnp.bfloat16)


def halves(pair, apart):
    rows = pair.shape[0] // 2
    apart[...] = pair[...].astype(jnp.float32)
    return [apart[pl.ds(at, rows), :] for at in (0, rows)]


def attend(query, key, value, key_count, head_width, out):
    per_slab = LANES // head_width
    factor = math.log2(math.e) / math.sqrt(head_width)
    query_total, key_total = query.shape[0], key.shape[0]
    head = lax.broadcasted_iota(jnp.int32, (query_total, LANES), 1) // head_width
    for at in range(0, query.shape[1], LANES):
        cut = slice(at, at + LANES)
        side = jnp.concatenate(
            [jnp.where(head == index, query[:, cut], 0) for index in range(per_slab)], axis=0
        )
        scores = lax.dot_general(key[:, cut], side, NT, preferred_element_type=jnp.float32)
        if key_count < key_total:
            place = lax.broadcasted_iota(jnp.int32, (key_total, 1), 0)
            scores = scores + jnp.where(place < key_count, 0.0, -1e30)
        top = jnp.max(scores, axis=0, keepdims=True)
        weights = jnp.exp2((scores - top) * factor)
        weights = weights * (1.0 / jnp.sum(weights, axis=0, keepdims=True))
        pooled = lax.dot_general(
            weights.astype(jnp.bfloat16), value[:, cut], TN, preferred_element_type=jnp.float32
        )
        mine = pooled[:query_total]
        for index in range(1, per_slab):
            mine = jnp.where(head == index, pooled[index * query_total : (index + 1) * query_total], mine)
        out[:, cut] = mine


def load_kernel(key, value, query, pair, near_query, near_key, near_value, apart, sems):
    targets = (near_key, near_value, near_query.at[0])
    copies = [
        pltpu.make_async_copy(source.at[0], target, sems.at[index])
        for index, (source, target) in enumerate(zip((key, value, query), targets))
    ]
    for copy in copies:
        copy.start()
    for copy in copies:
        copy.wait()
    pair[...] = stack_rows([near_key[...], near_value[...]], apart, near_key.shape[0])


def load(key, value, query):
    _, rows, width = key.shape
    return pl.pallas_call(
        load_kernel,
        out_shape=[near((2 * rows, width), key.dtype), near(query.shape, query.dtype)],
        in_specs=[FAR] * 3,
        out_specs=[VMEM] * 2,
        scratch_shapes=[
            near((rows, width), key.dtype),
            near((rows, width), key.dtype),
            near((2 * rows, width)),
            pltpu.SemaphoreType.DMA((3,)),
        ],
        name="load",
    )(far(key), far(value), far(query))


def fetch_kernel(*refs):
    count = len(refs) // 2
    far_refs, held, sems = refs[:count], refs[count : 2 * count], refs[-1]
    copies = [
        pltpu.make_async_copy(source, target, sems.at[index])
        for index, (source, target) in enumerate(zip(far_refs, held))
    ]
    for copy in copies:
        copy.start()
    for copy in copies:
        copy.wait()


def fetch(weights):
    return pl.pallas_call(
        fetch_kernel,
        out_shape=[pltpu.VMEM(matrix.shape, matrix.dtype) for matrix in weights],
        in_specs=[FAR] * len(weights),
        out_specs=[VMEM] * len(weights),
        scratch_shapes=[pltpu.SemaphoreType.DMA((len(weights),))],
        compiler_params=pltpu.CompilerParams(vmem_limit_bytes=32 << 20),
        cost_estimate=pl.CostEstimate(flops=0, bytes_accessed=len(weights) << 21, transcendentals=0),
        name="fetch",
    )(*map(far, weights))


def attention_kernel(head_width, query_count, earlier_count, block_count, *refs):
    queries, refs = refs[:query_count], refs[query_count:]
    blocks, refs = refs[:block_count], refs[block_count:]
    *refs, key_stage, value_stage, query_stage, apart = refs
    rows = blocks[0].shape[0] // 2
    if earlier_count:
        earlier, outs = refs[:earlier_count], refs[earlier_count:]
        query = queries[0][...]
    else:
        earlier, (*outs, stacked) = (), refs
        query = stack_rows([ref[0] for ref in queries], query_stage, rows)
        stacked[...] = query
    keys, values = zip(*[halves(ref, apart) for ref in blocks])
    key = stack_rows(keys, key_stage, rows)
    value = stack_rows(values, value_stage, rows)
    attend(query, key, value, block_count * rows, head_width, query_stage)
    for index, out in enumerate(outs):
        mine = query_stage[pl.ds(index * rows, rows), :]
        if earlier:
            out[...] = stack_rows([earlier[index][0], mine], apart, rows)
        else:
            out[0] = mine.astype(out.dtype)


def attention(queries, blocks, earlier=()):
    width = blocks[0].shape[1]
    rows = blocks[0].shape[0] // 2
    count = len(earlier) or len(queries)
    query_total, key_total = ceil_to(count * rows, 16), ceil_to(len(blocks) * rows, 16)
    flops = 4 * count * rows * len(blocks) * rows * width
    shape = jax.ShapeDtypeStruct((2 * rows, width) if earlier else (1, rows, width), jnp.bfloat16)
    first = not earlier
    kernel = functools.partial(
        attention_kernel, width // HEADS, len(queries), len(earlier), len(blocks)
    )
    return pl.pallas_call(
        kernel,
        out_shape=[shape] * count + [near((query_total, width), jnp.bfloat16)] * first,
        in_specs=[VMEM] * (len(queries) + len(blocks) + len(earlier)),
        out_specs=[VMEM] * (count + first),
        scratch_shapes=[near((key_total, width))] * 2
        + [near((query_total, width)), near((2 * rows, width))],
        compiler_params=pltpu.CompilerParams(vmem_limit_bytes=48 << 20),
        cost_estimate=pl.CostEstimate(flops=flops, bytes_accessed=1 << 20, transcendentals=0),
        name="attention",
    )(*queries, *blocks, *earlier)


def head_members(width, head_width):
    channel = lax.broadcasted_iota(jnp.int32, (width, LANES), 0) // head_width
    return (channel == lax.broadcasted_iota(jnp.int32, (width, LANES), 1)).astype(jnp.bfloat16)


def head_spread(width, head_width):
    channel = lax.broadcasted_iota(jnp.int32, (LANES, width), 1) // head_width
    return (channel == lax.broadcasted_iota(jnp.int32, (LANES, width), 0)).astype(jnp.bfloat16)


def project(rows, matrix):
    wide = jnp.dot(rows, matrix[...], preferred_element_type=jnp.float32)
    return wide.astype(jnp.bfloat16).astype(jnp.float32)


def score(query, pooled, w_key, head_width):
    path_key = project(pooled, w_key)
    pitch, width = query.shape
    product = jnp.concatenate(
        [path_key[at : at + pitch] * query for at in range(0, path_key.shape[0], pitch)], axis=0
    )
    member = head_members(width, head_width)
    high = product.astype(jnp.bfloat16)
    low = (product - high.astype(jnp.float32)).astype(jnp.bfloat16)
    scores = jnp.dot(high, member, preferred_element_type=jnp.float32) + jnp.dot(
        low, member, preferred_element_type=jnp.float32
    )
    return scores * (1.0 / math.sqrt(head_width))


def stack_pooled(refs, stage, apart, pitch):
    return stack_rows([half for ref in refs for half in halves(ref, apart)], stage, pitch)


def own_kernel(head_width, block, w_query, w_key, w_value, query, scores, values, stage, apart):
    rows, pitch = block.shape[0] // 2, query.shape[0]
    pooled = stack_pooled([block], stage, apart, pitch)
    query[...] = project(pooled[: ceil_to(rows, 16)], w_query)[:pitch]
    scores[...] = score(query[...], pooled, w_key, head_width)
    values[...] = project(pooled, w_value)


def part_kernel(head_width, block, query, w_key, w_value, scores, values, stage, apart):
    pooled = stack_pooled([block], stage, apart, query.shape[0])
    scores[...] = score(query[...], pooled, w_key, head_width)
    values[...] = project(pooled, w_value)


def last_kernel(head_width, earlier, count, *refs):
    blocks, (query, w_key, w_value), refs = refs[:count], refs[count : count + 3], refs[count + 3 :]
    score_refs, value_refs = refs[:earlier], refs[earlier : 2 * earlier]
    out, stage, apart = refs[-3:]
    pitch, width = query.shape
    pooled = stack_pooled(blocks, stage, apart, pitch)
    score_parts = [ref[...] for ref in score_refs] + [score(query[...], pooled, w_key, head_width)]
    value_parts = [ref[...] for ref in value_refs] + [project(pooled, w_value)]
    places = [
        (part, at) for part in range(earlier + 1) for at in range(0, score_parts[part].shape[0], pitch)
    ]
    scores = [score_parts[part][at : at + pitch] for part, at in places]
    top = functools.reduce(jnp.maximum, scores)
    scores = [jnp.exp(part - top) for part in scores]
    share = 1.0 / functools.reduce(jnp.add, scores)
    weights = jnp.concatenate([part * share for part in scores], axis=0).astype(jnp.bfloat16)
    weights = jnp.dot(weights, head_spread(width, head_width), preferred_element_type=jnp.float32)
    mixed = functools.reduce(
        jnp.add,
        [
            weights[index * pitch : (index + 1) * pitch] * value_parts[part][at : at + pitch]
            for index, (part, at) in enumerate(places)
        ],
    )
    out[0] = mixed[: blocks[0].shape[0] // 2].astype(jnp.bfloat16)


def near(shape, dtype=jnp.float32):
    return pltpu.VMEM(shape, dtype)


def mix_call(kernel, blocks, out_shape, operands, name):
    width = blocks[0].shape[1]
    rows = blocks[0].shape[0] // 2
    count = 2 * len(blocks)
    return pl.pallas_call(
        functools.partial(kernel, width // HEADS),
        out_shape=out_shape,
        in_specs=[VMEM] * (len(blocks) + len(operands)),
        out_specs=jax.tree.map(lambda _: VMEM, out_shape),
        scratch_shapes=[near((count * ceil_to(rows, 8), width)), near((2 * rows, width))],
        compiler_params=pltpu.CompilerParams(vmem_limit_bytes=32 << 20),
        cost_estimate=pl.CostEstimate(
            flops=4 * count * rows * width * width, bytes_accessed=4 << 20, transcendentals=0
        ),
        name=name,
    )(*blocks, *operands)


def part_shapes(block):
    width = block.shape[1]
    total = 2 * ceil_to(block.shape[0] // 2, 8)
    return [near((total, LANES)), near((total, width))]


def mix_own(block, weights):
    shapes = [near((ceil_to(block.shape[0] // 2, 8), block.shape[1])), *part_shapes(block)]
    query, *part = mix_call(own_kernel, [block], shapes, weights, "mix_own")
    return query, tuple(part)


def mix_part(block, query, w_key, w_value):
    return mix_call(part_kernel, [block], part_shapes(block), (query, w_key, w_value), "mix_part")


def mix_last(blocks, query, w_key, w_value, parts):
    scores, values = zip(*parts)
    return mix_call(
        lambda head_width, *refs: last_kernel(head_width, len(parts), len(blocks), *refs),
        blocks,
        jax.ShapeDtypeStruct((1, blocks[0].shape[0] // 2, blocks[0].shape[1]), blocks[0].dtype),
        (query, w_key, w_value, *scores, *values),
        "mix_last",
    )


def rounds(total):
    for step in range(1, total):
        if total & (total - 1) == 0:
            there = [(index, index ^ step) for index in range(total)]
        else:
            there = [(index, (index + step) % total) for index in range(total)]
        yield there, [(target, source) for source, target in there]


def chip_rounds(total):
    for there, back in rounds(total // 2):
        yield tuple(
            [(2 * source + core, 2 * target + core) for source, target in pairs for core in range(2)]
            for pairs in (there, back)
        )


def per_device(query_tokens, key_tokens, value_tokens, w_query, w_key, w_value):
    frame_total = lax.axis_size("frame")
    block_total = lax.axis_size("qblk")
    swap = [(index, index ^ 1) for index in range(frame_total)]
    own_block, near_query = load(key_tokens, value_tokens, query_tokens)
    steps = [there for there, _ in rounds(block_total)]
    order = steps[1:] + steps[:1]
    blocks = [own_block] + [lax.ppermute(own_block, "qblk", there) for there in order]
    paths = list(chip_rounds(frame_total))
    queries = [near_query] + [lax.ppermute(near_query, "frame", there) for there, _ in paths]
    w_query, w_key, w_value = fetch((w_query, w_key, w_value))
    *queries, w_query, w_key, w_value = lax.optimization_barrier((*queries, w_query, w_key, w_value))
    turned = [
        lax.optimization_barrier((block, *queries))[0] for block in blocks
    ]
    other_blocks = [lax.ppermute(block, "frame", swap) for block in turned]
    *own, query = attention(queries, blocks)
    pooled = attention([query], other_blocks, own)
    own_query, part = mix_own(pooled[0], (w_query, w_key, w_value))
    if not paths:
        return mix_last([pooled[0]], own_query, w_key, w_value, [])
    arrived = [
        lax.ppermute(block, "frame", back)
        for block, (_, back) in zip(pooled[1:], paths)
    ]
    parts = [part]
    for block in arrived[:1:-1]:
        parts.append(mix_part(block, own_query, w_key, w_value))
    return mix_last(arrived[:2], own_query, w_key, w_value, parts)


def solution(mesh):
    in_specs = (
        P("frame", "qblk", None),
        P("frame", "qblk", None),
        P("frame", "qblk", None),
        P(),
        P(),
        P(),
    )
    out_specs = P("frame", "qblk", None)
    return jax.shard_map(
        per_device, mesh=mesh, in_specs=in_specs, out_specs=out_specs, check_vma=False
    )
```
